256 devices in a mesh: ctx: 16 (over y_hi, x, core), tp: 16 (over y_lo, z).
Axes of the slice: x: 4, y: 4 (y_hi: 2, y_lo: 2; y = y_hi * 2 + y_lo), z: 8, core: 2. Of those that a mesh axis runs over, the one named last changes fastest.
Arguments:
- q_nope: bfloat16 [4096, 16384], P('ctx', 'tp'), may hold values from -6 to 6
- q_rope: bfloat16 [4096, 8192], P('ctx', 'tp'), may hold values from -6 to 6
- latent: bfloat16 [32768, 512], P('ctx'), may hold values from -6 to 6
- key_rope: bfloat16 [512, 4096], P('ctx'), may hold values from -6 to 6
- w_uk: bfloat16 [128, 128, 512], P('tp'), may hold values from -0.5 to 0.5
- w_uv: bfloat16 [128, 512, 128], P('tp'), may hold values from -0.25 to 0.25
- w_out: bfloat16 [16384, 7168], P('tp', 'ctx'), may hold values from -0.046875 to 0.046875
- block_lists: int32 [64, 32], P('ctx'), may hold values from 0 to 511, as said below
Outputs:
- attended: bfloat16 [4096, 7168], P('ctx', 'tp')
The draws below stay inside these ranges and needn't reach their ends.
Inputs may be any that keep to these rules, and one draw needn't show every extreme that they name: `block_lists`: each row lists 32 distinct blocks, none after the block of its own query block. Over the 4 rows of one ctx index, at most 6 distinct listed blocks lie among any one ctx index's 32 blocks of the cache, and exactly 6 among the first one's, the same ones in each of these rows, block 0 among them.
All inputs are finite; a program needn't handle non-finite values.
Results may differ from the reference program's by a relative error of at most 0.024.
Values may be sent and summed in bfloat16 or wider, within the bound.
A program may use at most 128 MiB of HBM per device.

```python
import math
import jax
import jax.numpy as jnp
from jax import lax

D = 7168
H = 128
DN = 128
DR = 64
DL = 512
DV = 128
BLK = 64
TOPB = 32
CAP = 6
QUERIES = 4096
CONTEXT = 32768
NBLK = 512
QBLOCKS = 64
QB_DEV = 4
BPD = 32
N_CTX = 16


def draw_q_nope(key, part):
    key = jax.random.fold_in(key, 1)
    values_drawn = jnp.clip(jax.random.normal(key, (QUERIES, H * DN), jnp.float32), -6.0, 6.0)
    return values_drawn.astype(jnp.bfloat16)


def draw_q_rope(key, part):
    key = jax.random.fold_in(key, 2)
    values_drawn = jnp.clip(jax.random.normal(key, (QUERIES, H, DR), jnp.float32), -6.0, 6.0)
    return values_drawn.reshape(QUERIES, H * DR).astype(jnp.bfloat16)


def draw_key_rope(key, part):
    key = jax.random.fold_in(key, 3)
    values_drawn = jnp.clip(jax.random.normal(key, (NBLK, BLK, DR), jnp.float32), -6.0, 6.0)
    return values_drawn.reshape(NBLK, BLK * DR).astype(jnp.bfloat16)


def draw_block_lists(key, part):
    key = jax.random.fold_in(key, 4)
    pool_key, pick_key = jax.random.split(key)
    owners = N_CTX
    local_index = jnp.arange(BPD, dtype=jnp.int32)
    raw_scores = jax.random.randint(pool_key, (owners, owners, BPD), 0, 1 << 20, dtype=jnp.int32)
    raw_scores = raw_scores * BPD + local_index[None, None, :]
    is_sink = (jnp.arange(owners, dtype=jnp.int32)[None, :, None] == 0) & (local_index[None, None, :] == 0)
    raw_scores = jnp.where(is_sink, jnp.int32(1 << 30), raw_scores)
    unused, chosen = lax.top_k(raw_scores, CAP)
    candidate = chosen.astype(jnp.int32) + (jnp.arange(owners, dtype=jnp.int32) * BPD)[None, :, None]
    sink_blocks = candidate[:, 0, :]
    pool_width = (owners - 1) * CAP
    others = candidate[:, 1:, :].reshape(owners, pool_width)
    query_block = NBLK - QBLOCKS + jnp.arange(QBLOCKS, dtype=jnp.int32).reshape(owners, QB_DEV)
    allowed = others[:, None, :] <= query_block[:, :, None]
    pick_scores = jax.random.randint(pick_key, (owners, QB_DEV, pool_width), 0, 1 << 20, dtype=jnp.int32)
    pick_scores = pick_scores * pool_width + jnp.arange(pool_width, dtype=jnp.int32)[None, None, :]
    pick_scores = jnp.where(allowed, pick_scores, -1)
    unused_too, pick_index = lax.top_k(pick_scores, TOPB - CAP)
    spread = jnp.broadcast_to(others[:, None, :], (owners, QB_DEV, pool_width))
    picked = jnp.take_along_axis(spread, pick_index.astype(jnp.int32), axis=2)
    listed = jnp.concatenate([jnp.broadcast_to(sink_blocks[:, None, :], (owners, QB_DEV, CAP)), picked], axis=2)
    return listed.reshape(QBLOCKS, TOPB).astype(jnp.int32)


def shard_levels(rng, extent, cuts, low, largest):
    level, own = 1.0, jax.random.fold_in(rng, 6)
    for position, blocks in cuts:
        steps = jnp.exp(jax.random.uniform(jax.random.fold_in(own, position), (blocks,), jnp.float32, low / len(cuts), largest / len(cuts)))
        level = level * jnp.repeat(steps, extent[position] // blocks).reshape([-1 if axis == position else 1 for axis in range(len(extent))])
    return level


def noise(key, extent, scale, limit, cuts=(), kind=jnp.bfloat16):
    entries = scale * jax.random.normal(key, extent, jnp.float32)
    if cuts:
        entries = entries * shard_levels(key, extent, cuts, -0.22, 0.18)
    return jnp.clip(entries, -limit, limit).astype(kind)


def setup_inputs(seed: int = 0) -> dict:
    seeds = jax.random.split(jax.random.key(seed), 9)
    return {
        "q_nope": draw_q_nope(jax.random.fold_in(seeds[8], 71), 0),
        "q_rope": draw_q_rope(jax.random.fold_in(seeds[8], 71), 0),
        "latent": noise(seeds[2], (CONTEXT, DL), 1.0, 6.0, ((0, 16),)),
        "key_rope": draw_key_rope(jax.random.fold_in(seeds[8], 71), 0),
        "w_uk": noise(seeds[4], (H, DN, DL), DN ** -0.5, 0.5, ((0, 16),)),
        "w_uv": noise(seeds[5], (H, DL, DV), DL ** -0.5, 0.25, ((0, 16),)),
        "w_out": noise(seeds[6], (H * DV, D), (H * DV) ** -0.5, 0.046875, ((0, 16), (1, 16))),
        "block_lists": draw_block_lists(jax.random.fold_in(seeds[8], 71), 0),
    }


mscale_sq = (0.1 * math.log(40.0) + 1.0) ** 2

def reference(q_nope, q_rope, latent, key_rope, w_uk, w_uv, w_out, block_lists):
    score_scale = mscale_sq / math.sqrt(DN + DR)
    q_absorbed = jnp.einsum('qhn,hnl->qhl', q_nope.reshape(QUERIES, H, DN).astype(jnp.float32), w_uk.astype(jnp.float32)).astype(jnp.bfloat16)
    q_rotary = q_rope.reshape(QUERIES, H, DR)
    latent_blocks = latent.reshape(NBLK, BLK, DL)
    rope_blocks = key_rope.reshape(NBLK, BLK, DR)
    token_offset = jnp.arange(BLK, dtype=jnp.int32)
    first_query = CONTEXT - QUERIES

    def attend(qblock):
        block_ids = block_lists[qblock]
        key_latent = latent_blocks[block_ids].reshape(TOPB * BLK, DL)
        key_part = rope_blocks[block_ids].reshape(TOPB * BLK, DR)
        key_position = (block_ids[:, None] * BLK + token_offset[None, :]).reshape(TOPB * BLK)
        query_latent = lax.dynamic_slice_in_dim(q_absorbed, qblock * BLK, BLK, 0).reshape(BLK * H, DL)
        query_rope = lax.dynamic_slice_in_dim(q_rotary, qblock * BLK, BLK, 0).reshape(BLK * H, DR)
        query_position = jnp.repeat(first_query + qblock * BLK + token_offset, H)
        scores = jnp.dot(query_latent, key_latent.T, preferred_element_type=jnp.float32)
        scores = scores + jnp.dot(query_rope, key_part.T, preferred_element_type=jnp.float32)
        scores = jnp.where(key_position[None, :] <= query_position[:, None], scores * score_scale, -1e+30)
        row_max = lax.optimization_barrier(jnp.max(scores, axis=1, keepdims=True))
        raised = jnp.exp(scores - row_max)
        weights = (raised / lax.optimization_barrier(jnp.sum(raised, axis=1, keepdims=True))).astype(jnp.bfloat16)
        latent_out = jnp.dot(weights, key_latent, preferred_element_type=jnp.float32).astype(jnp.bfloat16)
        latent_out = latent_out.reshape(BLK, H, DL)
        head_out = jnp.einsum('qhl,hlv->qhv', latent_out.astype(jnp.float32), w_uv.astype(jnp.float32)).astype(jnp.bfloat16)
        return head_out.reshape(BLK, H * DV)
    attended_heads = lax.map(attend, jnp.arange(QBLOCKS, dtype=jnp.int32)).reshape(QUERIES, H * DV)
    return jnp.dot(attended_heads, w_out, preferred_element_type=jnp.float32).astype(jnp.bfloat16)
```

```python
import functools
import math

import jax
import jax.numpy as jnp
from jax import lax
from jax.experimental import pallas as pl
from jax.experimental.pallas import tpu as pltpu
from jax.sharding import PartitionSpec as P

CAP = 6
N_CTX = 16
N_Z = 8
MESH = pl.DeviceIdType.MESH
bf16 = jnp.bfloat16
f32 = jnp.float32
VMEM_LIMIT = 56 * 1024 * 1024

mscale_sq = (0.1 * math.log(40.0) + 1.0) ** 2


def slot_tables(block_lists, owners, per_owner, capacity):
    block_count = owners * per_owner
    all_blocks = jnp.arange(block_count, dtype=jnp.int32)
    matches = block_lists[:, :, None] == all_blocks[None, None, :]
    present = jnp.any(matches, axis=(0, 1)).astype(jnp.int32).reshape(owners, per_owner)
    ranking = jnp.cumsum(present, axis=1) - 1
    slot_number = jnp.arange(capacity, dtype=jnp.int32)
    wanted = (present[:, None, :] == 1) & (ranking[:, None, :] == slot_number[None, :, None])
    local_index = jnp.arange(per_owner, dtype=jnp.int32)
    offsets = jnp.sum(jnp.where(wanted, local_index[None, None, :], 0), axis=2)
    slot_of_block = all_blocks // per_owner * capacity + ranking.reshape(block_count)
    slot_table = jnp.sum(jnp.where(matches, slot_of_block[None, None, :], 0), axis=2)
    return (offsets, slot_table)


def request_kernel(offsets, requested, send_sems, recv_sems):
    me = lax.axis_index("ctx")
    barrier = pltpu.get_barrier_semaphore()
    for k in range(1, N_CTX):
        pl.semaphore_signal(
            barrier, inc=1, device_id={"ctx": lax.rem(me + k, N_CTX)}, device_id_type=MESH
        )
    pl.semaphore_wait(barrier, N_CTX - 1)

    def copy(k):
        return pltpu.make_async_remote_copy(
            src_ref=offsets.at[lax.rem(me + k, N_CTX)],
            dst_ref=requested.at[me],
            send_sem=send_sems.at[k],
            recv_sem=recv_sems.at[k],
            device_id={"ctx": lax.rem(me + k, N_CTX)},
            device_id_type=MESH,
        )

    for k in range(1, N_CTX):
        copy(k).start()
    requested[me] = offsets[me]
    for k in range(1, N_CTX):
        copy(k).wait_send()
        pltpu.make_async_remote_copy(
            src_ref=offsets.at[me],
            dst_ref=requested.at[lax.rem(me + N_CTX - k, N_CTX)],
            send_sem=send_sems.at[k],
            recv_sem=recv_sems.at[k],
            device_id={"ctx": lax.rem(me + k, N_CTX)},
            device_id_type=MESH,
        ).wait_recv()


def exchange_requests(offsets):
    padded = jnp.pad(offsets[:, None, :], ((0, 0), (0, 7), (0, 128 - CAP)))
    got = pl.pallas_call(
        request_kernel,
        out_shape=jax.ShapeDtypeStruct(padded.shape, jnp.int32),
        in_specs=[pl.BlockSpec(memory_space=pltpu.VMEM)],
        out_specs=pl.BlockSpec(memory_space=pltpu.VMEM),
        scratch_shapes=[
            pltpu.SemaphoreType.DMA((N_CTX,)),
            pltpu.SemaphoreType.DMA((N_CTX,)),
        ],
        compiler_params=pltpu.CompilerParams(collective_id=1, has_side_effects=True),
    )(padded)
    return got[:, 0, :CAP]


DIRECT = 2


def pick_kernel(requested, place, latent, rope, direct, shared, ropes, sems):
    z = place[0]
    for c in range(N_CTX):
        for s in range(DIRECT):
            pltpu.make_async_copy(latent.at[requested[c, s]], direct.at[c, s], sems.at[0]).start()
        mine = requested[c, DIRECT + lax.div(z, 2)]
        pltpu.make_async_copy(
            latent.at[mine, pl.ds(pl.multiple_of(lax.rem(z, 2) * 32, 32), 32)],
            shared.at[c],
            sems.at[1],
        ).start()
        for s in range(CAP):
            pltpu.make_async_copy(rope.at[requested[c, s]], ropes.at[c, s], sems.at[2]).start()
    pltpu.make_async_copy(direct, direct, sems.at[0]).wait()
    pltpu.make_async_copy(shared, shared, sems.at[1]).wait()
    pltpu.make_async_copy(ropes, ropes, sems.at[2]).wait()


def pick(requested, place, latent, rope):
    blk, dl = latent.shape[1:]
    any_spec = pl.BlockSpec(memory_space=pl.ANY)
    return pl.pallas_call(
        pick_kernel,
        out_shape=(
            jax.ShapeDtypeStruct((N_CTX, DIRECT, blk, dl), bf16),
            jax.ShapeDtypeStruct((N_CTX, blk // 2, dl), bf16),
            jax.ShapeDtypeStruct((N_CTX, CAP) + rope.shape[1:], bf16),
        ),
        grid_spec=pltpu.PrefetchScalarGridSpec(
            num_scalar_prefetch=2,
            grid=(),
            in_specs=[any_spec, any_spec],
            out_specs=(any_spec, any_spec, any_spec),
            scratch_shapes=[pltpu.SemaphoreType.DMA((3,))],
        ),
    )(requested, place, latent, rope)


def fetch_kernel(direct, shared, ropes, kv, rp, own_sems, ctx_send, ctx_recv, ring_send, ring_recv):
    me = lax.axis_index("ctx")
    t = lax.axis_index("tp")
    z = lax.rem(t, N_Z)
    base = t - z
    right = base + lax.rem(z + 1, N_Z)
    left = base + lax.rem(z + N_Z - 1, N_Z)
    barrier = pltpu.get_barrier_semaphore()
    for k in range(1, N_CTX):
        pl.semaphore_signal(
            barrier, inc=1, device_id={"ctx": lax.rem(me + k, N_CTX)}, device_id_type=MESH
        )
    for peer in (left, right):
        pl.semaphore_signal(barrier, inc=1, device_id={"tp": peer}, device_id_type=MESH)
    pl.semaphore_wait(barrier, N_CTX + 1)

    def share(owners, zz):
        rows = pl.ds(pl.multiple_of(lax.rem(zz, 2) * 32, 32), 32)
        return kv.at[owners, DIRECT + lax.div(zz, 2), rows]

    def to_ctx(kind, k, owner):
        peer = lax.rem(me + k, N_CTX)
        src, dst = (
            (shared.at[peer], share(owner, z)),
            (direct.at[peer], kv.at[owner, pl.ds(0, DIRECT)]),
            (ropes.at[peer], rp.at[owner]),
        )[kind]
        return pltpu.make_async_remote_copy(
            src_ref=src,
            dst_ref=dst,
            send_sem=ctx_send.at[kind, k],
            recv_sem=ctx_recv.at[kind, k],
            device_id={"ctx": peer},
            device_id_type=MESH,
        )

    for kind in range(3):
        for k in range(1, N_CTX):
            to_ctx(kind, k, me).start()
    own = [
        pltpu.make_async_copy(shared.at[me], share(me, z), own_sems.at[0]),
        pltpu.make_async_copy(direct.at[me], kv.at[me, pl.ds(0, DIRECT)], own_sems.at[1]),
        pltpu.make_async_copy(ropes.at[me], rp.at[me], own_sems.at[2]),
    ]
    for copy in own:
        copy.start()
    own[0].wait()
    for k in range(1, N_CTX):
        to_ctx(0, k, lax.rem(me + N_CTX - k, N_CTX)).wait_recv()

    def ring(direction, step, zz):
        owners = pl.ds(0, N_CTX)
        if step == 3:
            owners = pl.ds(direction * (N_CTX // 2), N_CTX // 2)
        return pltpu.make_async_remote_copy(
            src_ref=share(owners, zz),
            dst_ref=share(owners, zz),
            send_sem=ring_send.at[direction, step],
            recv_sem=ring_recv.at[direction, step],
            device_id={"tp": (right, left)[direction]},
            device_id_type=MESH,
        )

    for step in range(4):
        ring(0, step, lax.rem(z + N_Z - step, N_Z)).start()
        ring(1, step, lax.rem(z + step, N_Z)).start()
        ring(0, step, lax.rem(z + N_Z - step - 1, N_Z)).wait_recv()
        ring(1, step, lax.rem(z + step + 1, N_Z)).wait_recv()
    for kind in (1, 2):
        own[kind].wait()
        for k in range(1, N_CTX):
            to_ctx(kind, k, lax.rem(me + N_CTX - k, N_CTX)).wait_recv()
    for kind in range(3):
        for k in range(1, N_CTX):
            to_ctx(kind, k, me).wait_send()
    for step in range(4):
        ring(0, step, z).wait_send()
        ring(1, step, z).wait_send()


def fetch(direct, shared, ropes):
    blk, dl = direct.shape[2:]
    any_spec = pl.BlockSpec(memory_space=pl.ANY)
    dma = pltpu.SemaphoreType.DMA
    return pl.pallas_call(
        fetch_kernel,
        out_shape=(
            jax.ShapeDtypeStruct((N_CTX, CAP, blk, dl), bf16),
            jax.ShapeDtypeStruct(ropes.shape, bf16),
        ),
        in_specs=[any_spec] * 3,
        out_specs=(any_spec, any_spec),
        scratch_shapes=[
            dma((3,)),
            dma((3, N_CTX)),
            dma((3, N_CTX)),
            dma((2, 4)),
            dma((2, 4)),
        ],
        compiler_params=pltpu.CompilerParams(collective_id=2, has_side_effects=True),
    )(direct, shared, ropes)


def attend_kernel(
    slots, lists, place, q_nope, q_rope, w_uk, w_uv, kv, rp, out, qbuf, kbuf, rbuf, obuf, sems
):
    heads, dn, dl = w_uk.shape
    dv = w_uv.shape[2]
    blocks, blk = kbuf.shape[1:3]
    keys = blocks * blk
    rows = heads * blk
    dr = q_rope.shape[1] // heads
    qb = pl.program_id(0)
    steps = pl.num_programs(0)
    buf = lax.rem(qb, 2)
    log2_scale = mscale_sq / math.sqrt(dn + dr) * math.log2(math.e)

    def load(step, into):
        for j in range(blocks):
            slot = slots[step, j]
            pltpu.make_async_copy(
                kv.at[slot], kbuf.at[into, j, :, pl.ds(0, dl)], sems.at[0, into]
            ).start()
            pltpu.make_async_copy(rp.at[slot], rbuf.at[into, j], sems.at[1, into]).start()

    @pl.when(qb == 0)
    def _():
        load(0, 0)
        lane = lax.broadcasted_iota(jnp.int32, (q_rope.shape[0], 128), 1)
        for h in range(heads):
            up = jnp.dot(q_nope[:, h * dn : (h + 1) * dn], w_uk[h], preferred_element_type=f32)
            qbuf[:, h, :, 0:dl] = up.astype(bf16).reshape(-1, blk, dl)
            pair = q_rope[:, h // 2 * 128 : h // 2 * 128 + 128]
            if h % 2:
                pair = jnp.concatenate([pair[:, 64:], pair[:, :64]], axis=1)
            pair = jnp.where(lane < dr, pair, jnp.zeros_like(pair))
            qbuf[:, h, :, dl : dl + 128] = pair.reshape(-1, blk, 128)

    @pl.when(qb + 1 < steps)
    def _():
        load(qb + 1, 1 - buf)

    whole = kbuf.at[buf, :, :, pl.ds(0, dl)]
    pltpu.make_async_copy(whole, whole, sems.at[0, buf]).wait()
    pltpu.make_async_copy(rbuf.at[buf], rbuf.at[buf], sems.at[1, buf]).wait()
    pairs = rbuf[buf]
    swapped = jnp.concatenate([pairs[:, :, 64:], pairs[:, :, :64]], axis=2)
    lane = lax.broadcasted_iota(jnp.int32, pairs.shape, 2)
    zero = jnp.zeros_like(pairs)
    kbuf[buf, :, 0 : blk // 2, dl : dl + 128] = jnp.where(lane < dr, pairs, zero)
    kbuf[buf, :, blk // 2 : blk, dl : dl + 128] = jnp.where(lane < dr, swapped, zero)

    own_block = place[1] + qb
    own_at = jnp.int32(-1000)
    for j in range(blocks):
        own_at = jnp.where(lists[qb, j] == own_block, j, own_at)
    ahead = lax.broadcasted_iota(jnp.int32, (blk, keys), 1) - own_at * blk
    row = lax.broadcasted_iota(jnp.int32, (blk, keys), 0)
    bias = jnp.where((ahead > row) & (ahead < blk), f32(-1e30), f32(0.0))

    key = kbuf[buf].reshape(keys, dl + 128)
    value = key[:, 0:dl]
    part = 4
    for first in range(0, heads, part):
        query = qbuf[qb, first : first + part].reshape(part * blk, dl + 128)
        scores = lax.dot_general(query, key, (((1,), (1,)), ((), ())), preferred_element_type=f32)
        scores = (scores.reshape(part, blk, keys) + bias[None]).reshape(part * blk, keys)
        top = jnp.max(scores, axis=1, keepdims=True)
        raised = jnp.exp2((scores - top) * log2_scale)
        total = jnp.sum(raised, axis=1, keepdims=True)
        mixed = jnp.dot(raised.astype(bf16), value, preferred_element_type=f32)
        mixed = (mixed / total).astype(bf16).reshape(part, blk, dl)
        obuf[first : first + part, pl.ds(pl.multiple_of(qb * blk, blk), blk), :] = mixed

    @pl.when(qb + 1 == steps)
    def _():
        for h in range(heads):
            out[:, h * dv : (h + 1) * dv] = jnp.dot(
                obuf[h], w_uv[h], preferred_element_type=f32
            ).astype(bf16)


def attend(slots, lists, place, q_nope, q_rope, w_uk, w_uv, kv, rp):
    queries = q_nope.shape[0]
    heads, dn, dl = w_uk.shape
    dv = w_uv.shape[2]
    blk = kv.shape[1]
    steps, blocks = slots.shape
    vmem = pl.BlockSpec(memory_space=pltpu.VMEM)
    any_spec = pl.BlockSpec(memory_space=pl.ANY)
    return pl.pallas_call(
        attend_kernel,
        out_shape=jax.ShapeDtypeStruct((queries, heads * dv), bf16),
        grid_spec=pltpu.PrefetchScalarGridSpec(
            num_scalar_prefetch=3,
            grid=(steps,),
            in_specs=[vmem, vmem, vmem, vmem, any_spec, any_spec],
            out_specs=vmem,
            scratch_shapes=[
                pltpu.VMEM((steps, heads, blk, dl + 128), bf16),
                pltpu.VMEM((2, blocks, blk, dl + 128), bf16),
                pltpu.VMEM((2, blocks) + rp.shape[1:], bf16),
                pltpu.VMEM((heads, queries, dl), bf16),
                pltpu.SemaphoreType.DMA((2, 2)),
            ],
        ),
        compiler_params=pltpu.CompilerParams(
            dimension_semantics=("arbitrary",), vmem_limit_bytes=VMEM_LIMIT
        ),
    )(slots, lists, place, q_nope, q_rope, w_uk, w_uv, kv, rp)


def project_kernel(
    heads_in, w_all, out, w_buf, part, sent, got, cross, w_sems, send_sems, recv_sems, cross_sems
):
    t = lax.axis_index("tp")
    z = lax.rem(t, N_Z)
    y = lax.div(t, N_Z)
    base = t - z
    right = base + lax.rem(z + 1, N_Z)
    left = base + lax.rem(z + N_Z - 1, N_Z)
    over = lax.rem(t + N_Z, 2 * N_Z)
    half = heads_in.shape[0] // 2
    barrier = pltpu.get_barrier_semaphore()
    for peer in (left, right, over):
        pl.semaphore_signal(barrier, inc=1, device_id={"tp": peer}, device_id_type=MESH)

    order = [N_Z - 1, 1, N_Z - 2, 2, N_Z - 3, 3, 4, 0]

    def weights(i, yy):
        block = lax.rem(z + order[i], N_Z) + N_Z * yy
        return pltpu.make_async_copy(w_all.at[block], w_buf.at[block], w_sems.at[i, yy])

    for i in range(N_Z):
        for yy in range(2):
            weights(i, yy).start()
    pl.semaphore_wait(barrier, 3)

    def compute(i):
        zz = lax.rem(z + order[i], N_Z)
        for yy in range(2):
            weights(i, yy).wait()
            part[zz, yy] = jnp.dot(heads_in[...], w_buf[zz + N_Z * yy], preferred_element_type=f32)

    def ring(direction, step):
        return pltpu.make_async_remote_copy(
            src_ref=sent.at[direction, step],
            dst_ref=got.at[direction, step],
            send_sem=send_sems.at[direction, step],
            recv_sem=recv_sems.at[direction, step],
            device_id={"tp": (right, left)[direction]},
            device_id_type=MESH,
        )

    for step in range(N_Z - 1):
        if step < 3:
            compute(2 * step)
            compute(2 * step + 1)
        elif step < 5:
            compute(step + 3)
        for direction in range(2):
            to = lax.rem(z + (N_Z - 1 - step, 1 + step)[direction], N_Z)
            mine = part[to, :, direction * half : (direction + 1) * half, :]
            if step:
                ring(direction, step - 1).wait_recv()
                mine = mine + got[direction, step - 1].astype(f32)
            sent[direction, step] = mine.astype(bf16)
            ring(direction, step).start()
    for direction in range(2):
        ring(direction, N_Z - 2).wait_recv()
        rows = slice(direction * half, (direction + 1) * half)
        part[z, :, rows, :] = part[z, :, rows, :] + got[direction, N_Z - 2].astype(f32)
    cross[0] = part[z, 1 - y].astype(bf16)
    swap = pltpu.make_async_remote_copy(
        src_ref=cross.at[0],
        dst_ref=cross.at[1],
        send_sem=cross_sems.at[0],
        recv_sem=cross_sems.at[1],
        device_id={"tp": over},
        device_id_type=MESH,
    )
    swap.start()
    swap.wait()
    out[...] = (part[z, y] + cross[1].astype(f32)).astype(bf16)
    for step in range(N_Z - 1):
        for direction in range(2):
            ring(direction, step).wait_send()


def project(heads_in, w_all):
    queries = heads_in.shape[0]
    depth, width = w_all.shape[1:]
    vmem = pl.BlockSpec(memory_space=pltpu.VMEM)
    dma = pltpu.SemaphoreType.DMA
    ring = (2, N_Z - 1, 2, queries // 2, width)
    return pl.pallas_call(
        project_kernel,
        out_shape=jax.ShapeDtypeStruct((queries, width), bf16),
        in_specs=[vmem, pl.BlockSpec(memory_space=pl.ANY)],
        out_specs=vmem,
        scratch_shapes=[
            pltpu.VMEM((2 * N_Z, depth, width), bf16),
            pltpu.VMEM((N_Z, 2, queries, width), f32),
            pltpu.VMEM(ring, bf16),
            pltpu.VMEM(ring, bf16),
            pltpu.VMEM((2, queries, width), bf16),
            dma((N_Z, 2)),
            dma((2, N_Z - 1)),
            dma((2, N_Z - 1)),
            dma((2,)),
        ],
        compiler_params=pltpu.CompilerParams(
            collective_id=3, has_side_effects=True, vmem_limit_bytes=VMEM_LIMIT
        ),
    )(heads_in, w_all)


def per_device(q_nope, q_rope, latent, key_rope, w_uk, w_uv, w_out, block_lists):
    owners = lax.axis_size("ctx")
    local_heads, head_dim, latent_dim = w_uk.shape
    rope_dim = q_rope.shape[1] // local_heads
    per_owner, row_width = key_rope.shape
    block_len = row_width // rope_dim
    queries = q_nope.shape[0]
    w_all = lax.all_gather(w_out, "ctx", axis=0)
    offsets, slots = slot_tables(block_lists, owners, per_owner, CAP)
    requested = exchange_requests(offsets)
    blocks_before = per_owner * owners - queries // block_len * owners
    own_block = blocks_before + lax.axis_index("ctx") * (queries // block_len)
    place = jnp.stack([lax.rem(lax.axis_index("tp"), N_Z), own_block]).astype(jnp.int32)
    latent_blocks = latent.reshape(per_owner, block_len, latent_dim)
    rope_pairs = (
        key_rope.reshape(per_owner, 2, block_len // 2, rope_dim)
        .transpose(0, 2, 1, 3)
        .reshape(per_owner, block_len // 2, 2 * rope_dim)
    )
    kv, rp = fetch(*pick(requested, place, latent_blocks, rope_pairs))
    kv = kv.reshape(owners * CAP, block_len, latent_dim)
    rp = rp.reshape(owners * CAP, block_len // 2, 2 * rope_dim)
    heads_out = attend(slots, block_lists, place, q_nope, q_rope, w_uk, w_uv, kv, rp)
    return project(heads_out, w_all)


def solution(mesh):
    placed = (
        P("ctx", "tp"),
        P("ctx", "tp"),
        P("ctx", None),
        P("ctx", None),
        P("tp", None, None),
        P("tp", None, None),
        P("tp", "ctx"),
        P("ctx", None),
    )
    return jax.shard_map(
        per_device, mesh=mesh, in_specs=placed, out_specs=P("ctx", "tp"), check_vma=False
    )
```

```python
import functools
import math

import jax
import jax.numpy as jnp
from jax import lax
from jax.experimental import pallas as pl
from jax.experimental.pallas import tpu as pltpu
from jax.sharding import PartitionSpec as P

CAP = 6
N_CTX = 16
N_Z = 8
MESH = pl.DeviceIdType.MESH
bf16 = jnp.bfloat16
f32 = jnp.float32
VMEM_LIMIT = 56 * 1024 * 1024

mscale_sq = (0.1 * math.log(40.0) + 1.0) ** 2


def slot_tables(block_lists, owners, per_owner, capacity, rank):
    block_count = owners * per_owner
    all_blocks = jnp.arange(block_count, dtype=jnp.int32)
    matches = block_lists[:, :, None] == all_blocks[None, None, :]
    present = jnp.any(matches, axis=(0, 1)).astype(jnp.int32).reshape(owners, per_owner)
    ranking = jnp.cumsum(present, axis=1) - 1
    slot_number = jnp.arange(capacity, dtype=jnp.int32)
    wanted = (present[:, None, :] == 1) & (ranking[:, None, :] == slot_number[None, :, None])
    local_index = jnp.arange(per_owner, dtype=jnp.int32)
    offsets = jnp.sum(jnp.where(wanted, local_index[None, None, :], 0), axis=2)
    slot_of_block = (rank[:, None] * capacity + ranking).reshape(block_count)
    slot_table = jnp.sum(jnp.where(matches, slot_of_block[None, None, :], 0), axis=2)
    return (offsets, slot_table)


RANKS = [(0, 0), (1, 0), (3, 0), (0, 1), (2, 0), (1, 1), (2, 1), (3, 1)]
N_DIRECT = 8


def shifted(me, dx, dy, dk):
    y, x, core = lax.div(me, 8), lax.rem(lax.div(me, 2), 4), lax.rem(me, 2)
    return lax.rem(y + dy, 2) * 8 + lax.rem(x + dx, 4) * 2 + lax.rem(core + dk, 2)


def owner_of(me, rank):
    dx, dy = RANKS[rank // 2]
    return shifted(me, dx, dy, rank % 2)


def asker_of(me, rank):
    dx, dy = RANKS[rank // 2]
    return shifted(me, (4 - dx) % 4, dy, rank % 2)


def rank_table(me):
    owner = jnp.arange(N_CTX, dtype=jnp.int32)
    dy = (owner // 8 - me // 8 + 2) % 2
    dx = (owner // 2 % 4 - me // 2 % 4 + 4) % 4
    dk = (owner - me + N_CTX) % 2
    rank = jnp.zeros_like(owner)
    for i, (x, y) in enumerate(RANKS):
        rank = jnp.where((dx == x) & (dy == y), 2 * i + dk, rank)
    return rank


def fetch_kernel(
    offsets,
    latent,
    rope,
    kv,
    rp,
    got,
    asked,
    direct,
    shared,
    ropes,
    far_ropes,
    ask_send,
    ask_recv,
    ask_local,
    own_sems,
    ctx_send,
    ctx_recv,
    ring_send,
    ring_recv,
):
    me = lax.axis_index("ctx")
    t = lax.axis_index("tp")
    z = lax.rem(t, N_Z)
    base = t - z
    right = base + lax.rem(z + 1, N_Z)
    left = base + lax.rem(z + N_Z - 1, N_Z)
    blk = latent.shape[1]
    share_rows = CAP * blk // N_Z
    barrier = pltpu.get_barrier_semaphore()
    for rank in range(1, N_CTX):
        pl.semaphore_signal(
            barrier, inc=1, device_id={"ctx": owner_of(me, rank)}, device_id_type=MESH
        )
    for peer in (left, right):
        pl.semaphore_signal(barrier, inc=1, device_id={"tp": peer}, device_id_type=MESH)
    pl.semaphore_wait(barrier, N_CTX + 1)

    def ask(rank):
        return pltpu.make_async_remote_copy(
            src_ref=offsets.at[owner_of(me, rank)],
            dst_ref=got.at[rank],
            send_sem=ask_send.at[rank],
            recv_sem=ask_recv.at[rank],
            device_id={"ctx": owner_of(me, rank)},
            device_id_type=MESH,
        )

    order = list(range(N_DIRECT, N_CTX)) + list(range(1, N_DIRECT))
    for rank in order:
        ask(rank).start()
    got[0] = offsets[me]

    def to_scalars(rank):
        return pltpu.make_async_copy(got.at[rank], asked.at[rank], ask_local.at[rank])

    far_dy = lax.div(z + 6, 8)
    far_dx = 2 * (1 - far_dy) + far_dy * lax.div(z, 2)
    far_asker = shifted(me, lax.rem(4 - far_dx, 4), far_dy, lax.rem(z, 2))

    def send(kind, rank):
        if rank >= N_DIRECT:
            src = shared.at[rank - N_DIRECT]
            rows = pl.ds(pl.multiple_of(z * share_rows, share_rows), share_rows)
            dst = kv.at[rank, rows]
        else:
            src, dst = ((direct.at[rank], kv.at[rank]), (ropes.at[rank], rp.at[rank]))[kind]
        return pltpu.make_async_remote_copy(
            src_ref=src,
            dst_ref=dst,
            send_sem=ctx_send.at[kind, rank],
            recv_sem=ctx_recv.at[kind, rank],
            device_id={"ctx": asker_of(me, rank)},
            device_id_type=MESH,
        )

    def send_far_ropes():
        return pltpu.make_async_remote_copy(
            src_ref=far_ropes,
            dst_ref=rp.at[N_DIRECT + z],
            send_sem=ctx_send.at[1, N_DIRECT],
            recv_sem=ctx_recv.at[1, N_DIRECT],
            device_id={"ctx": far_asker},
            device_id_type=MESH,
        )

    for rank in order:
        ask(rank).wait_recv()
        to_scalars(rank).start()
    to_scalars(0).start()
    for rank in range(N_DIRECT, N_CTX):
        to_scalars(rank).wait()
        for i in range(share_rows // 16):
            group = z * (share_rows // 16) + i
            block = asked[rank, 0, lax.div(group, blk // 16)]
            rows = pl.ds(pl.multiple_of(lax.rem(group, blk // 16) * 16, 16), 16)
            shared[rank - N_DIRECT, 16 * i : 16 * i + 16, :] = latent[block, rows, :]
        send(0, rank).start()
    half = blk // 2
    for s in range(CAP):
        far_ropes[s * half : (s + 1) * half, :] = rope[asked[N_DIRECT + z, 0, s]]
    send_far_ropes().start()
    for rank in list(range(1, N_DIRECT)) + [0]:
        to_scalars(rank).wait()
        for s in range(CAP):
            block = asked[rank, 0, s]
            direct[rank, s * blk : (s + 1) * blk, :] = latent[block]
            ropes[rank, s * half : (s + 1) * half, :] = rope[block]
        if rank:
            send(0, rank).start()
            send(1, rank).start()
    own = [
        pltpu.make_async_copy(direct.at[0], kv.at[0], own_sems.at[0]),
        pltpu.make_async_copy(ropes.at[0], rp.at[0], own_sems.at[1]),
    ]
    for copy in own:
        copy.start()

    def ring(direction, step, piece, zz):
        if piece == 2:
            part = rp.at[N_DIRECT + zz]
        else:
            rows = pl.ds(pl.multiple_of(zz * share_rows, share_rows), share_rows)
            part = kv.at[pl.ds(N_DIRECT + 4 * piece, 4), rows]
        return pltpu.make_async_remote_copy(
            src_ref=part,
            dst_ref=part,
            send_sem=ring_send.at[direction, step, piece],
            recv_sem=ring_recv.at[direction, step, piece],
            device_id={"tp": (right, left)[direction]},
            device_id_type=MESH,
        )

    def pieces(direction, step):
        return (0, 1, 2) if step < 3 else ((0,), (1, 2))[direction]

    def seen_from(direction, step):
        return lax.rem(z + (N_Z - step if direction == 0 else step), N_Z)

    for step in range(4):
        for piece in range(3):
            if step == 0:
                if piece == 2:
                    send_far_ropes().wait_recv()
                else:
                    for rank in range(N_DIRECT + 4 * piece, N_DIRECT + 4 * piece + 4):
                        send(0, rank).wait_recv()
            for direction in range(2):
                if step:
                    ring(direction, step - 1, piece, seen_from(direction, step)).wait_recv()
                if piece in pieces(direction, step):
                    ring(direction, step, piece, seen_from(direction, step)).start()
    for direction in range(2):
        for piece in pieces(direction, 3):
            ring(direction, 3, piece, seen_from(direction, 4)).wait_recv()
    for copy in own:
        copy.wait()
    for rank in range(1, N_CTX):
        ask(rank).wait_send()
        send(0, rank).wait_send()
        if rank < N_DIRECT:
            send(0, rank).wait_recv()
            send(1, rank).wait_recv()
            send(1, rank).wait_send()
    send_far_ropes().wait_send()
    for direction in range(2):
        for step in range(4):
            for piece in pieces(direction, step):
                ring(direction, step, piece, seen_from(direction, step)).wait_send()


def fetch(offsets, latent, rope):
    blk, dl = latent.shape[1:]
    half, pair = rope.shape[1:]
    offsets = jnp.pad(offsets[:, None, :], ((0, 0), (0, 7), (0, 128 - CAP)))
    any_spec = pl.BlockSpec(memory_space=pl.ANY)
    vmem = pl.BlockSpec(memory_space=pltpu.VMEM)
    dma = pltpu.SemaphoreType.DMA
    return pl.pallas_call(
        fetch_kernel,
        out_shape=(
            jax.ShapeDtypeStruct((N_CTX, CAP * blk, dl), bf16),
            jax.ShapeDtypeStruct((N_CTX, CAP * half, pair), bf16),
        ),
        in_specs=[vmem] * 3,
        out_specs=(any_spec, any_spec),
        scratch_shapes=[
            pltpu.VMEM(offsets.shape, jnp.int32),
            pltpu.SMEM(offsets.shape, jnp.int32),
            pltpu.VMEM((N_DIRECT, CAP * blk, dl), bf16),
            pltpu.VMEM((N_CTX - N_DIRECT, CAP * blk // N_Z, dl), bf16),
            pltpu.VMEM((N_DIRECT, CAP * half, pair), bf16),
            pltpu.VMEM((CAP * half, pair), bf16),
            dma((N_CTX,)),
            dma((N_CTX,)),
            dma((N_CTX,)),
            dma((2,)),
            dma((2, N_CTX)),
            dma((2, N_CTX)),
            dma((2, 4, 3)),
            dma((2, 4, 3)),
        ],
        compiler_params=pltpu.CompilerParams(
            collective_id=2, has_side_effects=True, vmem_limit_bytes=VMEM_LIMIT
        ),
    )(offsets, latent, rope)


def attend_kernel(
    slots, lists, place, q_nope, q_rope, w_uk, w_uv, kv, rp, out, qbuf, kbuf, rbuf, obuf, sems
):
    heads, dn, dl = w_uk.shape
    dv = w_uv.shape[2]
    blocks, blk = kbuf.shape[1:3]
    keys = blocks * blk
    rows = heads * blk
    dr = q_rope.shape[1] // heads
    qb = pl.program_id(0)
    steps = pl.num_programs(0)
    buf = lax.rem(qb, 2)
    log2_scale = mscale_sq / math.sqrt(dn + dr) * math.log2(math.e)

    def load(step, into):
        for j in range(blocks):
            slot = slots[step, j]
            pltpu.make_async_copy(
                kv.at[slot], kbuf.at[into, j, :, pl.ds(0, dl)], sems.at[0, into]
            ).start()
            pltpu.make_async_copy(rp.at[slot], rbuf.at[into, j], sems.at[1, into]).start()

    @pl.when(qb == 0)
    def _():
        load(0, 0)
        lane = lax.broadcasted_iota(jnp.int32, (q_rope.shape[0], 128), 1)
        for h in range(heads):
            up = jnp.dot(q_nope[:, h * dn : (h + 1) * dn], w_uk[h], preferred_element_type=f32)
            qbuf[:, h, :, 0:dl] = up.astype(bf16).reshape(-1, blk, dl)
            pair = q_rope[:, h // 2 * 128 : h // 2 * 128 + 128]
            if h % 2:
                pair = jnp.concatenate([pair[:, 64:], pair[:, :64]], axis=1)
            pair = jnp.where(lane < dr, pair, jnp.zeros_like(pair))
            qbuf[:, h, :, dl : dl + 128] = pair.reshape(-1, blk, 128)

    @pl.when(qb + 1 < steps)
    def _():
        load(qb + 1, 1 - buf)

    whole = kbuf.at[buf, :, :, pl.ds(0, dl)]
    pltpu.make_async_copy(whole, whole, sems.at[0, buf]).wait()
    pltpu.make_async_copy(rbuf.at[buf], rbuf.at[buf], sems.at[1, buf]).wait()
    pairs = rbuf[buf]
    swapped = jnp.concatenate([pairs[:, :, 64:], pairs[:, :, :64]], axis=2)
    lane = lax.broadcasted_iota(jnp.int32, pairs.shape, 2)
    zero = jnp.zeros_like(pairs)
    kbuf[buf, :, 0 : blk // 2, dl : dl + 128] = jnp.where(lane < dr, pairs, zero)
    kbuf[buf, :, blk // 2 : blk, dl : dl + 128] = jnp.where(lane < dr, swapped, zero)

    own_block = place[0] + qb
    own_at = jnp.int32(-1000)
    for j in range(blocks):
        own_at = jnp.where(lists[qb, j] == own_block, j, own_at)
    ahead = lax.broadcasted_iota(jnp.int32, (blk, keys), 1) - own_at * blk
    row = lax.broadcasted_iota(jnp.int32, (blk, keys), 0)
    bias = jnp.where((ahead > row) & (ahead < blk), f32(-1e30), f32(0.0))

    key = kbuf[buf].reshape(keys, dl + 128)
    value = key[:, 0:dl]
    part = 4
    for first in range(0, heads, part):
        query = qbuf[qb, first : first + part].reshape(part * blk, dl + 128)
        scores = lax.dot_general(query, key, (((1,), (1,)), ((), ())), preferred_element_type=f32)
        scores = (scores.reshape(part, blk, keys) + bias[None]).reshape(part * blk, keys)
        top = jnp.max(scores, axis=1, keepdims=True)
        raised = jnp.exp2((scores - top) * log2_scale)
        total = jnp.sum(raised, axis=1, keepdims=True)
        mixed = jnp.dot(raised.astype(bf16), value, preferred_element_type=f32)
        mixed = (mixed / total).astype(bf16).reshape(part, blk, dl)
        obuf[first : first + part, pl.ds(pl.multiple_of(qb * blk, blk), blk), :] = mixed

    @pl.when(qb + 1 == steps)
    def _():
        for h in range(heads):
            out[:, h * dv : (h + 1) * dv] = jnp.dot(
                obuf[h], w_uv[h], preferred_element_type=f32
            ).astype(bf16)


def attend(slots, lists, place, q_nope, q_rope, w_uk, w_uv, kv, rp):
    queries = q_nope.shape[0]
    heads, dn, dl = w_uk.shape
    dv = w_uv.shape[2]
    blk = kv.shape[1]
    steps, blocks = slots.shape
    vmem = pl.BlockSpec(memory_space=pltpu.VMEM)
    any_spec = pl.BlockSpec(memory_space=pl.ANY)
    return pl.pallas_call(
        attend_kernel,
        out_shape=jax.ShapeDtypeStruct((queries, heads * dv), bf16),
        grid_spec=pltpu.PrefetchScalarGridSpec(
            num_scalar_prefetch=3,
            grid=(steps,),
            in_specs=[vmem, vmem, vmem, vmem, any_spec, any_spec],
            out_specs=vmem,
            scratch_shapes=[
                pltpu.VMEM((steps, heads, blk, dl + 128), bf16),
                pltpu.VMEM((2, blocks, blk, dl + 128), bf16),
                pltpu.VMEM((2, blocks) + rp.shape[1:], bf16),
                pltpu.VMEM((heads, queries, dl), bf16),
                pltpu.SemaphoreType.DMA((2, 2)),
            ],
        ),
        compiler_params=pltpu.CompilerParams(
            dimension_semantics=("arbitrary",), vmem_limit_bytes=VMEM_LIMIT
        ),
    )(slots, lists, place, q_nope, q_rope, w_uk, w_uv, kv, rp)


def project_kernel(
    heads_in, w_all, out, w_buf, part, sent, got, cross, w_sems, send_sems, recv_sems, cross_sems
):
    t = lax.axis_index("tp")
    z = lax.rem(t, N_Z)
    y = lax.div(t, N_Z)
    base = t - z
    right = base + lax.rem(z + 1, N_Z)
    left = base + lax.rem(z + N_Z - 1, N_Z)
    over = lax.rem(t + N_Z, 2 * N_Z)
    half = heads_in.shape[0] // 2
    barrier = pltpu.get_barrier_semaphore()
    for peer in (left, right, over):
        pl.semaphore_signal(barrier, inc=1, device_id={"tp": peer}, device_id_type=MESH)

    order = [N_Z - 1, 1, N_Z - 2, 2, N_Z - 3, 3, 4, 0]

    def weights(i, yy):
        block = lax.rem(z + order[i], N_Z) + N_Z * yy
        return pltpu.make_async_copy(w_all.at[block], w_buf.at[block], w_sems.at[i, yy])

    for i in range(N_Z):
        for yy in range(2):
            weights(i, yy).start()
    pl.semaphore_wait(barrier, 3)

    def compute(i):
        zz = lax.rem(z + order[i], N_Z)
        for yy in range(2):
            weights(i, yy).wait()
            part[zz, yy] = jnp.dot(heads_in[...], w_buf[zz + N_Z * yy], preferred_element_type=f32)

    def ring(direction, step):
        return pltpu.make_async_remote_copy(
            src_ref=sent.at[direction, step],
            dst_ref=got.at[direction, step],
            send_sem=send_sems.at[direction, step],
            recv_sem=recv_sems.at[direction, step],
            device_id={"tp": (right, left)[direction]},
            device_id_type=MESH,
        )

    for step in range(N_Z - 1):
        if step < 3:
            compute(2 * step)
            compute(2 * step + 1)
        elif step < 5:
            compute(step + 3)
        for direction in range(2):
            to = lax.rem(z + (N_Z - 1 - step, 1 + step)[direction], N_Z)
            mine = part[to, :, direction * half : (direction + 1) * half, :]
            if step:
                ring(direction, step - 1).wait_recv()
                mine = mine + got[direction, step - 1].astype(f32)
            sent[direction, step] = mine.astype(bf16)
            ring(direction, step).start()
    for direction in range(2):
        ring(direction, N_Z - 2).wait_recv()
        rows = slice(direction * half, (direction + 1) * half)
        part[z, :, rows, :] = part[z, :, rows, :] + got[direction, N_Z - 2].astype(f32)
    cross[0] = part[z, 1 - y].astype(bf16)
    swap = pltpu.make_async_remote_copy(
        src_ref=cross.at[0],
        dst_ref=cross.at[1],
        send_sem=cross_sems.at[0],
        recv_sem=cross_sems.at[1],
        device_id={"tp": over},
        device_id_type=MESH,
    )
    swap.start()
    swap.wait()
    out[...] = (part[z, y] + cross[1].astype(f32)).astype(bf16)
    for step in range(N_Z - 1):
        for direction in range(2):
            ring(direction, step).wait_send()


def project(heads_in, w_all):
    queries = heads_in.shape[0]
    depth, width = w_all.shape[1:]
    vmem = pl.BlockSpec(memory_space=pltpu.VMEM)
    dma = pltpu.SemaphoreType.DMA
    ring = (2, N_Z - 1, 2, queries // 2, width)
    return pl.pallas_call(
        project_kernel,
        out_shape=jax.ShapeDtypeStruct((queries, width), bf16),
        in_specs=[vmem, pl.BlockSpec(memory_space=pl.ANY)],
        out_specs=vmem,
        scratch_shapes=[
            pltpu.VMEM((2 * N_Z, depth, width), bf16),
            pltpu.VMEM((N_Z, 2, queries, width), f32),
            pltpu.VMEM(ring, bf16),
            pltpu.VMEM(ring, bf16),
            pltpu.VMEM((2, queries, width), bf16),
            dma((N_Z, 2)),
            dma((2, N_Z - 1)),
            dma((2, N_Z - 1)),
            dma((2,)),
        ],
        compiler_params=pltpu.CompilerParams(
            collective_id=3, has_side_effects=True, vmem_limit_bytes=VMEM_LIMIT
        ),
    )(heads_in, w_all)


def per_device(q_nope, q_rope, latent, key_rope, w_uk, w_uv, w_out, block_lists):
    owners = lax.axis_size("ctx")
    local_heads, head_dim, latent_dim = w_uk.shape
    rope_dim = q_rope.shape[1] // local_heads
    per_owner, row_width = key_rope.shape
    block_len = row_width // rope_dim
    queries = q_nope.shape[0]
    w_all = lax.all_gather(w_out, "ctx", axis=0)
    me = lax.axis_index("ctx")
    offsets, slots = slot_tables(block_lists, owners, per_owner, CAP, rank_table(me))
    blocks_before = per_owner * owners - queries // block_len * owners
    own_block = blocks_before + me * (queries // block_len)
    place = own_block[None].astype(jnp.int32)
    latent_blocks = latent.reshape(per_owner, block_len, latent_dim)
    rope_pairs = (
        key_rope.reshape(per_owner, 2, block_len // 2, rope_dim)
        .transpose(0, 2, 1, 3)
        .reshape(per_owner, block_len // 2, 2 * rope_dim)
    )
    kv, rp = fetch(offsets, latent_blocks, rope_pairs)
    kv = kv.reshape(owners * CAP, block_len, latent_dim)
    rp = rp.reshape(owners * CAP, block_len // 2, 2 * rope_dim)
    heads_out = attend(slots, block_lists, place, q_nope, q_rope, w_uk, w_uv, kv, rp)
    return project(heads_out, w_all)


def solution(mesh):
    placed = (
        P("ctx", "tp"),
        P("ctx", "tp"),
        P("ctx", None),
        P("ctx", None),
        P("tp", None, None),
        P("tp", None, None),
        P("tp", "ctx"),
        P("ctx", None),
    )
    return jax.shard_map(
        per_device, mesh=mesh, in_specs=placed, out_specs=P("ctx", "tp"), check_vma=False
    )
```

```python
import functools
import math

import jax
import jax.numpy as jnp
from jax import lax
from jax.experimental import pallas as pl
from jax.experimental.pallas import tpu as pltpu
from jax.sharding import PartitionSpec as P

CAP = 6
N_CTX = 16
N_Z = 8
MESH = pl.DeviceIdType.MESH
bf16 = jnp.bfloat16
f32 = jnp.float32
VMEM_LIMIT = 60 * 1024 * 1024

mscale_sq = (0.1 * math.log(40.0) + 1.0) ** 2


def slot_tables(block_lists, owners, per_owner, capacity, rank):
    block_count = owners * per_owner
    all_blocks = jnp.arange(block_count, dtype=jnp.int32)
    matches = block_lists[:, :, None] == all_blocks[None, None, :]
    present = jnp.any(matches, axis=(0, 1)).astype(jnp.int32).reshape(owners, per_owner)
    ranking = jnp.cumsum(present, axis=1) - 1
    slot_number = jnp.arange(capacity, dtype=jnp.int32)
    wanted = (present[:, None, :] == 1) & (ranking[:, None, :] == slot_number[None, :, None])
    local_index = jnp.arange(per_owner, dtype=jnp.int32)
    offsets = jnp.sum(jnp.where(wanted, local_index[None, None, :], 0), axis=2)
    rank_of_block = jnp.broadcast_to(rank[:, None], (owners, per_owner)).reshape(block_count)
    ranks = jnp.sum(jnp.where(matches, rank_of_block[None, None, :], 0), axis=2)
    places = jnp.sum(jnp.where(matches, ranking.reshape(block_count)[None, None, :], 0), axis=2)
    return (offsets, ranks, places)


RANKS = [(0, 0), (1, 0), (3, 0), (0, 1), (2, 0), (1, 1), (2, 1), (3, 1)]
N_DIRECT = 8


def shifted(me, dx, dy, dk):
    y, x, core = lax.div(me, 8), lax.rem(lax.div(me, 2), 4), lax.rem(me, 2)
    return lax.rem(y + dy, 2) * 8 + lax.rem(x + dx, 4) * 2 + lax.rem(core + dk, 2)


def owner_of(me, rank):
    dx, dy = RANKS[rank // 2]
    return shifted(me, dx, dy, rank % 2)


def asker_of(me, rank):
    dx, dy = RANKS[rank // 2]
    return shifted(me, (4 - dx) % 4, dy, rank % 2)


def rank_table(me):
    owner = jnp.arange(N_CTX, dtype=jnp.int32)
    dy = (owner // 8 - me // 8 + 2) % 2
    dx = (owner // 2 % 4 - me // 2 % 4 + 4) % 4
    dk = (owner - me + N_CTX) % 2
    rank = jnp.zeros_like(owner)
    for i, (x, y) in enumerate(RANKS):
        rank = jnp.where((dx == x) & (dy == y), 2 * i + dk, rank)
    return rank


def layer_kernel(
    offsets,
    picked,
    latent,
    rope,
    q_nope,
    q_rope,
    w_uk,
    w_uv,
    w_out,
    out,
    got,
    asked,
    direct,
    shared,
    ropes,
    far_ropes,
    kv,
    rp,
    ask_send,
    ask_recv,
    ask_local,
    own_sems,
    ctx_send,
    ctx_recv,
    ring_send,
    ring_recv,
    qbuf,
    kbuf,
    obuf,
    heads_out,
    head_send,
    head_recv,
    w_buf,
    w_send,
    w_recv,
    part,
    sent,
    arrived,
    sum_send,
    sum_recv,
    last_sent,
    last_got,
    last_send,
    last_recv,
):
    me = lax.axis_index("ctx")
    t = lax.axis_index("tp")
    z = lax.rem(t, N_Z)
    y_lo = lax.div(t, N_Z)
    y_hi = lax.div(me, 8)
    x_core = lax.rem(me, 8)
    base = t - z
    right = base + lax.rem(z + 1, N_Z)
    left = base + lax.rem(z + N_Z - 1, N_Z)
    opposite = shifted(me, 0, 1, 0)
    other_core = shifted(me, 0, 0, 1)
    x_next = (shifted(me, 1, 0, 0), shifted(me, 3, 0, 0))
    home = y_hi * N_Z + z
    blk = 16 * latent.shape[1]
    half_blk = blk // 2
    block_groups = blk // 16
    share_groups = CAP * block_groups // N_Z
    heads, dn, dl = w_uk.shape
    dv = w_uv.shape[2]
    dr = q_rope.shape[1] // heads
    steps, blocks = picked.shape[0], picked.shape[1] // 2
    keys = blocks * blk
    queries = q_nope.shape[0]
    width = w_out.shape[0]
    half_width = width // 2

    barrier = pltpu.get_barrier_semaphore()
    for rank in range(1, N_CTX):
        pl.semaphore_signal(
            barrier, inc=1, device_id={"ctx": owner_of(me, rank)}, device_id_type=MESH
        )
    across = lax.rem(t + N_Z, 2 * N_Z)
    for peer in (left, right, across):
        pl.semaphore_signal(barrier, inc=1, device_id={"tp": peer}, device_id_type=MESH)
    pl.semaphore_signal(
        barrier, inc=1, device_id={"ctx": opposite, "tp": across}, device_id_type=MESH
    )

    own_w = pltpu.make_async_copy(w_out, w_buf.at[x_core], own_sems.at[2])
    own_w.start()
    pl.semaphore_wait(barrier, N_CTX + 3)


    def ask(rank):
        return pltpu.make_async_remote_copy(
            src_ref=offsets.at[owner_of(me, rank)],
            dst_ref=got.at[rank],
            send_sem=ask_send.at[rank],
            recv_sem=ask_recv.at[rank],
            device_id={"ctx": owner_of(me, rank)},
            device_id_type=MESH,
        )

    order = list(range(N_DIRECT, N_CTX)) + list(range(1, N_DIRECT))
    for rank in order:
        ask(rank).start()
    got[0] = offsets[me]

    def to_scalars(rank):
        return pltpu.make_async_copy(got.at[rank], asked.at[rank], ask_local.at[rank])

    far_dy = lax.div(z + 6, 8)
    far_dx = 2 * (1 - far_dy) + far_dy * lax.div(z, 2)
    far_asker = shifted(me, lax.rem(4 - far_dx, 4), far_dy, lax.rem(z, 2))

    def send(kind, rank):
        if rank >= N_DIRECT:
            src = shared.at[rank - N_DIRECT]
            dst = kv.at[rank, pl.ds(z * share_groups, share_groups)]
        else:
            src, dst = ((direct.at[rank], kv.at[rank]), (ropes.at[rank], rp.at[rank]))[kind]
        return pltpu.make_async_remote_copy(
            src_ref=src,
            dst_ref=dst,
            send_sem=ctx_send.at[kind, rank],
            recv_sem=ctx_recv.at[kind, rank],
            device_id={"ctx": asker_of(me, rank)},
            device_id_type=MESH,
        )

    def send_far_ropes():
        return pltpu.make_async_remote_copy(
            src_ref=far_ropes,
            dst_ref=rp.at[N_DIRECT + z],
            send_sem=ctx_send.at[1, N_DIRECT],
            recv_sem=ctx_recv.at[1, N_DIRECT],
            device_id={"ctx": far_asker},
            device_id_type=MESH,
        )

    for rank in order:
        ask(rank).wait_recv()
        to_scalars(rank).start()
    to_scalars(0).start()
    for rank in range(N_DIRECT, N_CTX):
        to_scalars(rank).wait()
        for i in range(share_groups):
            group = z * share_groups + i
            block = asked[rank, 0, lax.div(group, block_groups)]
            shared[rank - N_DIRECT, i] = latent[block, lax.rem(group, block_groups)]
        send(0, rank).start()
    for s in range(CAP):
        far_ropes[s] = rope[asked[N_DIRECT + z, 0, s]]
    send_far_ropes().start()
    for rank in list(range(1, N_DIRECT)) + [0]:
        to_scalars(rank).wait()
        for s in range(CAP):
            block = asked[rank, 0, s]
            direct[rank, s * block_groups : (s + 1) * block_groups] = latent[block]
            ropes[rank, s] = rope[block]
        if rank:
            send(0, rank).start()
            send(1, rank).start()
    own = [
        pltpu.make_async_copy(direct.at[0], kv.at[0], own_sems.at[0]),
        pltpu.make_async_copy(ropes.at[0], rp.at[0], own_sems.at[1]),
    ]
    for copy in own:
        copy.start()


    def ring(direction, step, piece, zz):
        if piece == 2:
            moved = rp.at[N_DIRECT + zz]
        else:
            moved = kv.at[pl.ds(N_DIRECT + 4 * piece, 4), pl.ds(zz * share_groups, share_groups)]
        return pltpu.make_async_remote_copy(
            src_ref=moved,
            dst_ref=moved,
            send_sem=ring_send.at[direction, step, piece],
            recv_sem=ring_recv.at[direction, step, piece],
            device_id={"tp": (right, left)[direction]},
            device_id_type=MESH,
        )

    def pieces(direction, step):
        return (0, 1, 2) if step < 3 else ((0,), (1, 2))[direction]

    def seen_from(direction, step):
        return lax.rem(z + (N_Z - step if direction == 0 else step), N_Z)


    def column(dx):
        return lax.rem(x_core + 2 * dx, 8)

    def move_w(i):
        source = (0, 0, 3, 1, 0, 3, 1, 2)[i]
        rows = pl.ds((i - 2) * half_width, half_width) if i in (2, 3) else pl.ds(0, width)
        peer = other_core if i >= 4 else x_next[i % 2]
        block = w_buf.at[column(source), rows]
        return pltpu.make_async_remote_copy(
            src_ref=block,
            dst_ref=block,
            send_sem=w_send.at[i],
            recv_sem=w_recv.at[i],
            device_id={"ctx": peer},
            device_id_type=MESH,
        )

    for step in range(4):
        for piece in range(3):
            if step == 0:
                if piece == 2:
                    send_far_ropes().wait_recv()
                else:
                    for rank in range(N_DIRECT + 4 * piece, N_DIRECT + 4 * piece + 4):
                        send(0, rank).wait_recv()
            for direction in range(2):
                if step:
                    ring(direction, step - 1, piece, seen_from(direction, step)).wait_recv()
                if piece in pieces(direction, step):
                    ring(direction, step, piece, seen_from(direction, step)).start()
        if step == 0:
            lane = lax.broadcasted_iota(jnp.int32, (queries, 128), 1)
            for h in range(heads):
                up = jnp.dot(q_nope[:, h * dn : (h + 1) * dn], w_uk[h], preferred_element_type=f32)
                qbuf[:, h, :, 0:dl] = up.astype(bf16).reshape(-1, blk, dl)
                pair = q_rope[:, h // 2 * 128 : h // 2 * 128 + 128]
                if h % 2:
                    pair = jnp.concatenate([pair[:, 64:], pair[:, :64]], axis=1)
                pair = jnp.where(lane < dr, pair, jnp.zeros_like(pair))
                qbuf[:, h, :, dl : dl + 128] = pair.reshape(-1, blk, 128)
        if step == 2:
            own_w.wait()
            for i in (0, 1, 4):
                move_w(i).start()
    for direction in range(2):
        for piece in pieces(direction, 3):
            ring(direction, 3, piece, seen_from(direction, 4)).wait_recv()
    for copy in own:
        copy.wait()
    for rank in range(1, N_DIRECT):
        send(0, rank).wait_recv()
        send(1, rank).wait_recv()


    log2_scale = mscale_sq / math.sqrt(dn + dr) * math.log2(math.e)

    def send_heads(qb):
        rows = pl.ds(pl.multiple_of(qb * blk, blk), blk)
        return pltpu.make_async_remote_copy(
            src_ref=heads_out.at[0, rows],
            dst_ref=heads_out.at[1, rows],
            send_sem=head_send.at[qb],
            recv_sem=head_recv.at[qb],
            device_id={"ctx": opposite},
            device_id_type=MESH,
        )

    def attend(qb, carry):
        lane = lax.broadcasted_iota(jnp.int32, (half_blk, 128), 1)
        for j in range(blocks):
            rank, place = picked[qb, j], picked[qb, blocks + j]
            for i in range(block_groups):
                first = j * blk + 16 * i
                kbuf[first : first + 16, 0:dl] = kv[rank, place * block_groups + i]
            pair = rp[rank, place]
            swapped = jnp.concatenate([pair[:, 64:], pair[:, :64]], axis=1)
            zero = jnp.zeros_like(pair)
            kbuf[j * blk : j * blk + half_blk, dl : dl + 128] = jnp.where(lane < dr, pair, zero)
            kbuf[j * blk + half_blk : (j + 1) * blk, dl : dl + 128] = jnp.where(
                lane < dr, swapped, zero
            )
        ahead = lax.broadcasted_iota(jnp.int32, (blk, keys), 1) - picked[qb, 2 * blocks]
        row = lax.broadcasted_iota(jnp.int32, (blk, keys), 0)
        bias = jnp.where((ahead > row) & (ahead < blk), f32(-1e30), f32(0.0))

        key = kbuf[...]
        value = key[:, 0:dl]
        group = 4
        for first in range(0, heads, group):
            query = qbuf[qb, first : first + group].reshape(group * blk, dl + 128)
            scores = lax.dot_general(
                query, key, (((1,), (1,)), ((), ())), preferred_element_type=f32
            )
            scores = (scores.reshape(group, blk, keys) + bias[None]).reshape(group * blk, keys)
            top = jnp.max(scores, axis=1, keepdims=True)
            raised = jnp.exp2((scores - top) * log2_scale)
            total = jnp.sum(raised, axis=1, keepdims=True)
            mixed = jnp.dot(raised.astype(bf16), value, preferred_element_type=f32)
            obuf[first : first + group] = (mixed / total).astype(bf16).reshape(group, blk, dl)
        rows = pl.ds(pl.multiple_of(qb * blk, blk), blk)
        for h in range(heads):
            heads_out[0, rows, h * dv : (h + 1) * dv] = jnp.dot(
                obuf[h], w_uv[h], preferred_element_type=f32
            ).astype(bf16)
        send_heads(qb).start()

        @pl.when(qb == 1)
        def _():
            move_w(0).wait_recv()
            move_w(1).wait_recv()
            for i in (2, 3, 5, 6):
                move_w(i).start()

        return carry

    lax.fori_loop(0, steps, attend, 0)
    move_w(2).wait_recv()
    move_w(3).wait_recv()
    move_w(7).start()
    for i in (4, 5, 6, 7):
        move_w(i).wait_recv()


    def compute(dz, side):
        zz = lax.rem(z + dz, N_Z)
        part[side, zz] = lax.dot_general(
            w_buf[zz], heads_out[side], (((1,), (1,)), ((), ())), preferred_element_type=f32
        )

    def half(direction):
        return slice(direction * half_width, (direction + 1) * half_width)

    def pass_on(direction, step, side):
        return pltpu.make_async_remote_copy(
            src_ref=sent.at[direction, step, side],
            dst_ref=arrived.at[direction, step, side],
            send_sem=sum_send.at[direction, step, side],
            recv_sem=sum_recv.at[direction, step, side],
            device_id={"tp": (right, left)[direction]},
            device_id_type=MESH,
        )

    for step in range(N_Z - 1):
        for side in range(2):
            if step == 0 and side == 1:
                for qb in range(steps):
                    send_heads(qb).wait_recv()
            if step < 3:
                compute(N_Z - 1 - step, side)
                compute(1 + step, side)
            elif step < 5:
                compute((4, 0)[step - 3], side)
            for direction in range(2):
                to = lax.rem(z + (N_Z - 1 - step, 1 + step)[direction], N_Z)
                mine = part[side, to, half(direction), :]
                if step:
                    pass_on(direction, step - 1, side).wait_recv()
                    mine = mine + arrived[direction, step - 1, side].astype(f32)
                sent[direction, step, side] = mine.astype(bf16)
                pass_on(direction, step, side).start()

    def total_of(side, direction):
        return part[side, z, half(direction), :] + arrived[direction, N_Z - 2, side].astype(f32)

    is_home = y_lo == y_hi

    def send_last(side):
        slot = jnp.where(is_home, 0, 1) if side else 0
        return pltpu.make_async_remote_copy(
            src_ref=last_sent.at[side],
            dst_ref=last_got.at[slot],
            send_sem=last_send.at[side],
            recv_sem=last_recv.at[slot],
            device_id={"ctx": opposite if side else me, "tp": home},
            device_id_type=MESH,
        )

    def landed(slot):
        return pltpu.make_async_remote_copy(
            src_ref=last_sent.at[slot],
            dst_ref=last_got.at[slot],
            send_sem=last_send.at[slot],
            recv_sem=last_recv.at[slot],
            device_id={"ctx": opposite, "tp": home},
            device_id_type=MESH,
        )

    for side in (1, 0):
        for direction in range(2):
            pass_on(direction, N_Z - 2, side).wait_recv()
            last_sent[side, half(direction), :] = total_of(side, direction).astype(bf16)
        if side:
            send_last(1).start()

    @pl.when(jnp.logical_not(is_home))
    def _():
        send_last(0).start()
        landed(0).wait_recv()
        landed(1).wait_recv()
        out[...] = (last_got[0].astype(f32) + last_got[1].astype(f32)).astype(bf16)
        send_last(0).wait_send()

    @pl.when(is_home)
    def _():
        landed(0).wait_recv()
        for direction in range(2):
            mine = total_of(0, direction) + last_got[0, half(direction), :].astype(f32)
            out[half(direction), :] = mine.astype(bf16)

    for rank in range(1, N_CTX):
        ask(rank).wait_send()
        send(0, rank).wait_send()
        if rank < N_DIRECT:
            send(1, rank).wait_send()
    send_far_ropes().wait_send()
    for direction in range(2):
        for step in range(4):
            for piece in pieces(direction, step):
                ring(direction, step, piece, seen_from(direction, step)).wait_send()
        for step in range(N_Z - 1):
            for side in range(2):
                pass_on(direction, step, side).wait_send()
    for i in range(8):
        move_w(i).wait_send()
    for qb in range(steps):
        send_heads(qb).wait_send()
    send_last(1).wait_send()


def layer(offsets, picked, latent, rope, q_nope, q_rope, w_uk, w_uv, w_out):
    block_groups = latent.shape[1]
    blk = 16 * block_groups
    half, pair = rope.shape[1:]
    queries = q_nope.shape[0]
    heads, dn, dl = w_uk.shape
    dv = w_uv.shape[2]
    steps, blocks = picked.shape[0], picked.shape[1] // 2
    width, depth = w_out.shape
    offsets = jnp.pad(offsets[:, None, :], ((0, 0), (0, 7), (0, 128 - CAP)))
    vmem = pl.BlockSpec(memory_space=pltpu.VMEM)
    smem = pl.BlockSpec(memory_space=pltpu.SMEM)
    dma = pltpu.SemaphoreType.DMA
    sums = (2, N_Z - 1, 2, width // 2, queries)
    return pl.pallas_call(
        layer_kernel,
        out_shape=jax.ShapeDtypeStruct((width, queries), bf16),
        in_specs=[vmem, smem] + [vmem] * 6 + [pl.BlockSpec(memory_space=pl.ANY)],
        out_specs=vmem,
        scratch_shapes=[
            pltpu.VMEM(offsets.shape, jnp.int32),
            pltpu.SMEM(offsets.shape, jnp.int32),
            pltpu.VMEM((N_DIRECT, CAP * block_groups, 16, dl), bf16),
            pltpu.VMEM((N_CTX - N_DIRECT, CAP * block_groups // N_Z, 16, dl), bf16),
            pltpu.VMEM((N_DIRECT, CAP, half, pair), bf16),
            pltpu.VMEM((CAP, half, pair), bf16),
            pltpu.VMEM((N_CTX, CAP * block_groups, 16, dl), bf16),
            pltpu.VMEM((N_CTX, CAP, half, pair), bf16),
            dma((N_CTX,)),
            dma((N_CTX,)),
            dma((N_CTX,)),
            dma((3,)),
            dma((2, N_CTX)),
            dma((2, N_CTX)),
            dma((2, 4, 3)),
            dma((2, 4, 3)),
            pltpu.VMEM((steps, heads, blk, dl + 128), bf16),
            pltpu.VMEM((blocks * blk, dl + 128), bf16),
            pltpu.VMEM((heads, blk, dl), bf16),
            pltpu.VMEM((2, queries, heads * dv), bf16),
            dma((steps,)),
            dma((steps,)),
            pltpu.VMEM((N_Z, width, depth), bf16),
            dma((8,)),
            dma((8,)),
            pltpu.VMEM((2, N_Z, width, queries), f32),
            pltpu.VMEM(sums, bf16),
            pltpu.VMEM(sums, bf16),
            dma(sums[:3]),
            dma(sums[:3]),
            pltpu.VMEM((2, width, queries), bf16),
            pltpu.VMEM((2, width, queries), bf16),
            dma((2,)),
            dma((2,)),
        ],
        compiler_params=pltpu.CompilerParams(
            collective_id=2, has_side_effects=True, vmem_limit_bytes=VMEM_LIMIT
        ),
    )(offsets, picked, latent, rope, q_nope, q_rope, w_uk, w_uv, w_out)


def per_device(q_nope, q_rope, latent, key_rope, w_uk, w_uv, w_out, block_lists):
    owners = lax.axis_size("ctx")
    local_heads, head_dim, latent_dim = w_uk.shape
    rope_dim = q_rope.shape[1] // local_heads
    per_owner, row_width = key_rope.shape
    block_len = row_width // rope_dim
    me = lax.axis_index("ctx")
    offsets, ranks, places = slot_tables(block_lists, owners, per_owner, CAP, rank_table(me))
    steps, blocks = block_lists.shape
    own_block = owners * (per_owner - steps) + me * steps + jnp.arange(steps, dtype=jnp.int32)
    is_own = block_lists == own_block[:, None]
    own_at = jnp.sum(
        jnp.where(is_own, (jnp.arange(blocks, dtype=jnp.int32) * block_len + (1 << 20))[None, :], 0), axis=1
    ) - (1 << 20)
    picked = jnp.concatenate([ranks, places, own_at[:, None]], axis=1)
    latent_blocks = latent.reshape(per_owner, block_len // 16, 16, latent_dim)
    rope_pairs = (
        key_rope.reshape(per_owner, 2, block_len // 2, rope_dim)
        .transpose(0, 2, 1, 3)
        .reshape(per_owner, block_len // 2, 2 * rope_dim)
    )
    return layer(
        offsets, picked, latent_blocks, rope_pairs, q_nope, q_rope, w_uk, w_uv, w_out.T
    ).T


def solution(mesh):
    placed = (
        P("ctx", "tp"),
        P("ctx", "tp"),
        P("ctx", None),
        P("ctx", None),
        P("tp", None, None),
        P("tp", None, None),
        P("tp", "ctx"),
        P("ctx", None),
    )
    return jax.shard_map(
        per_device, mesh=mesh, in_specs=placed, out_specs=P("ctx", "tp"), check_vma=False
    )
```

```python
import functools
import math

import jax
import jax.numpy as jnp
from jax import lax
from jax.experimental import pallas as pl
from jax.experimental.pallas import tpu as pltpu
from jax.sharding import PartitionSpec as P

CAP = 6
N_CTX = 16
N_Z = 8
MESH = pl.DeviceIdType.MESH
bf16 = jnp.bfloat16
f32 = jnp.float32
VMEM_LIMIT = 60 * 1024 * 1024

mscale_sq = (0.1 * math.log(40.0) + 1.0) ** 2


def slot_tables(block_lists, owners, per_owner, capacity, rank):
    block_count = owners * per_owner
    all_blocks = jnp.arange(block_count, dtype=jnp.int32)
    matches = block_lists[:, :, None] == all_blocks[None, None, :]
    present = jnp.any(matches, axis=(0, 1)).astype(jnp.int32).reshape(owners, per_owner)
    ranking = jnp.cumsum(present, axis=1) - 1
    slot_number = jnp.arange(capacity, dtype=jnp.int32)
    wanted = (present[:, None, :] == 1) & (ranking[:, None, :] == slot_number[None, :, None])
    local_index = jnp.arange(per_owner, dtype=jnp.int32)
    offsets = jnp.sum(jnp.where(wanted, local_index[None, None, :], 0), axis=2)
    rank_of_block = jnp.broadcast_to(rank[:, None], (owners, per_owner)).reshape(block_count)
    ranks = jnp.sum(jnp.where(matches, rank_of_block[None, None, :], 0), axis=2)
    places = jnp.sum(jnp.where(matches, ranking.reshape(block_count)[None, None, :], 0), axis=2)
    return (offsets, ranks, places)


RANKS = [(0, 0), (1, 0), (3, 0), (0, 1), (1, 1), (3, 1), (2, 0), (2, 1)]
N_DIRECT = 8


def shifted(me, dx, dy, dk):
    y, x, core = lax.div(me, 8), lax.rem(lax.div(me, 2), 4), lax.rem(me, 2)
    return lax.rem(y + dy, 2) * 8 + lax.rem(x + dx, 4) * 2 + lax.rem(core + dk, 2)


def owner_of(me, rank):
    dx, dy = RANKS[rank // 2]
    return shifted(me, dx, dy, rank % 2)


def asker_of(me, rank):
    dx, dy = RANKS[rank // 2]
    return shifted(me, (4 - dx) % 4, dy, rank % 2)


def rank_table(me):
    owner = jnp.arange(N_CTX, dtype=jnp.int32)
    dy = (owner // 8 - me // 8 + 2) % 2
    dx = (owner // 2 % 4 - me // 2 % 4 + 4) % 4
    dk = (owner - me + N_CTX) % 2
    rank = jnp.zeros_like(owner)
    for i, (x, y) in enumerate(RANKS):
        rank = jnp.where((dx == x) & (dy == y), 2 * i + dk, rank)
    return rank


def layer_kernel(
    offsets,
    picked,
    latent,
    rope,
    q_nope_in,
    q_rope_in,
    w_uk_in,
    w_uv_in,
    w_out,
    out,
    q_nope,
    q_rope,
    w_uk,
    w_uv,
    load_sems,
    got,
    asked,
    direct,
    shared,
    ropes,
    far_ropes,
    kv,
    rp,
    ask_send,
    ask_recv,
    ask_local,
    own_sems,
    ctx_send,
    ctx_recv,
    ring_send,
    ring_recv,
    qbuf,
    kbuf,
    heads_out,
    head_send,
    head_recv,
    w_buf,
    w_send,
    w_recv,
    part,
    sent,
    arrived,
    sum_send,
    sum_recv,
    last_sent,
    last_got,
    last_send,
    last_recv,
):
    me = lax.axis_index("ctx")
    t = lax.axis_index("tp")
    z = lax.rem(t, N_Z)
    y_lo = lax.div(t, N_Z)
    y_hi = lax.div(me, 8)
    x_core = lax.rem(me, 8)
    base = t - z
    right = base + lax.rem(z + 1, N_Z)
    left = base + lax.rem(z + N_Z - 1, N_Z)
    opposite = shifted(me, 0, 1, 0)
    other_core = shifted(me, 0, 0, 1)
    x_next = (shifted(me, 1, 0, 0), shifted(me, 3, 0, 0))
    home = y_hi * N_Z + z
    blk = 16 * latent.shape[1]
    half_blk = blk // 2
    block_groups = blk // 16
    share_groups = CAP * block_groups // N_Z
    heads, dn, dl = w_uk.shape
    dv = w_uv.shape[2]
    dr = q_rope.shape[1] // heads
    steps, blocks = picked.shape[0], picked.shape[1] // 2
    keys = blocks * blk
    queries = q_nope.shape[0]
    width = w_out.shape[0]
    half_width = width // 2

    barrier = pltpu.get_barrier_semaphore()
    for rank in range(1, N_CTX):
        pl.semaphore_signal(
            barrier, inc=1, device_id={"ctx": owner_of(me, rank)}, device_id_type=MESH
        )
    across = lax.rem(t + N_Z, 2 * N_Z)
    for peer in (left, right, across):
        pl.semaphore_signal(barrier, inc=1, device_id={"tp": peer}, device_id_type=MESH)
    pl.semaphore_signal(
        barrier, inc=1, device_id={"ctx": opposite, "tp": across}, device_id_type=MESH
    )

    own_w = pltpu.make_async_copy(w_out, w_buf.at[x_core], own_sems.at[2])
    own_w.start()
    loads = [
        pltpu.make_async_copy(src, dst, load_sems.at[i])
        for i, (src, dst) in enumerate(
            ((q_nope_in, q_nope), (q_rope_in, q_rope), (w_uk_in, w_uk), (w_uv_in, w_uv))
        )
    ]
    for copy in loads:
        copy.start()
    pl.semaphore_wait(barrier, N_CTX + 3)


    def ask(rank):
        return pltpu.make_async_remote_copy(
            src_ref=offsets.at[owner_of(me, rank)],
            dst_ref=got.at[rank],
            send_sem=ask_send.at[rank],
            recv_sem=ask_recv.at[rank],
            device_id={"ctx": owner_of(me, rank)},
            device_id_type=MESH,
        )

    order = list(range(N_DIRECT, N_CTX)) + list(range(1, N_DIRECT))
    for rank in order:
        ask(rank).start()
    got[0] = offsets[me]

    def to_scalars(rank):
        return pltpu.make_async_copy(got.at[rank], asked.at[rank], ask_local.at[rank])

    far_dy = jnp.where(lax.div(z, 2) == 2, 0, 1)
    far_dx = jnp.where(z < 4, 1 + 2 * lax.div(z, 2), 2)
    far_asker = shifted(me, lax.rem(4 - far_dx, 4), far_dy, lax.rem(z, 2))

    def send(kind, rank):
        if rank >= N_DIRECT:
            src = shared.at[rank - N_DIRECT]
            dst = kv.at[rank, pl.ds(z * share_groups, share_groups)]
        else:
            src, dst = ((direct.at[rank], kv.at[rank]), (ropes.at[rank], rp.at[rank]))[kind]
        return pltpu.make_async_remote_copy(
            src_ref=src,
            dst_ref=dst,
            send_sem=ctx_send.at[kind, rank],
            recv_sem=ctx_recv.at[kind, rank],
            device_id={"ctx": asker_of(me, rank)},
            device_id_type=MESH,
        )

    def send_far_ropes():
        return pltpu.make_async_remote_copy(
            src_ref=far_ropes,
            dst_ref=rp.at[N_DIRECT + z],
            send_sem=ctx_send.at[1, N_DIRECT],
            recv_sem=ctx_recv.at[1, N_DIRECT],
            device_id={"ctx": far_asker},
            device_id_type=MESH,
        )

    for rank in order:
        ask(rank).wait_recv()
        to_scalars(rank).start()
    to_scalars(0).start()
    for rank in range(N_DIRECT, N_CTX):
        to_scalars(rank).wait()
        for i in range(share_groups):
            group = z * share_groups + i
            block = asked[rank, 0, lax.div(group, block_groups)]
            shared[rank - N_DIRECT, i] = latent[block, lax.rem(group, block_groups)]
        send(0, rank).start()
    for s in range(CAP):
        far_ropes[s] = rope[asked[N_DIRECT + z, 0, s]]
    send_far_ropes().start()
    for rank in list(range(1, N_DIRECT)) + [0]:
        to_scalars(rank).wait()
        for s in range(CAP):
            block = asked[rank, 0, s]
            direct[rank, s * block_groups : (s + 1) * block_groups] = latent[block]
            ropes[rank, s] = rope[block]
        if rank:
            send(0, rank).start()
            send(1, rank).start()
    own = [
        pltpu.make_async_copy(direct.at[0], kv.at[0], own_sems.at[0]),
        pltpu.make_async_copy(ropes.at[0], rp.at[0], own_sems.at[1]),
    ]
    for copy in own:
        copy.start()


    def ring(direction, step, piece, zz):
        if piece == 2:
            moved = rp.at[N_DIRECT + zz]
        else:
            moved = kv.at[pl.ds(N_DIRECT + 4 * piece, 4), pl.ds(zz * share_groups, share_groups)]
        return pltpu.make_async_remote_copy(
            src_ref=moved,
            dst_ref=moved,
            send_sem=ring_send.at[direction, step, piece],
            recv_sem=ring_recv.at[direction, step, piece],
            device_id={"tp": (right, left)[direction]},
            device_id_type=MESH,
        )

    def pieces(direction, step):
        return (0, 1, 2) if step < 3 else ((0,), (1, 2))[direction]

    def seen_from(direction, step):
        return lax.rem(z + (N_Z - step if direction == 0 else step), N_Z)


    def column(dx):
        return lax.rem(x_core + 2 * dx, 8)

    def move_w(i):
        source = (0, 0, 3, 1, 0, 3, 1, 2)[i]
        rows = pl.ds((i - 2) * half_width, half_width) if i in (2, 3) else pl.ds(0, width)
        peer = other_core if i >= 4 else x_next[i % 2]
        block = w_buf.at[column(source), rows]
        return pltpu.make_async_remote_copy(
            src_ref=block,
            dst_ref=block,
            send_sem=w_send.at[i],
            recv_sem=w_recv.at[i],
            device_id={"ctx": peer},
            device_id_type=MESH,
        )

    for step in range(4):
        for piece in range(3):
            if step == 0:
                if piece == 2:
                    send_far_ropes().wait_recv()
                else:
                    for rank in range(N_DIRECT + 4 * piece, N_DIRECT + 4 * piece + 4):
                        send(0, rank).wait_recv()
            for direction in range(2):
                if step:
                    ring(direction, step - 1, piece, seen_from(direction, step)).wait_recv()
                if piece in pieces(direction, step):
                    ring(direction, step, piece, seen_from(direction, step)).start()
        if step == 0:
            for copy in loads:
                copy.wait()
            lane = lax.broadcasted_iota(jnp.int32, (queries, 128), 1)
            for h in range(heads):
                up = jnp.dot(q_nope[:, h * dn : (h + 1) * dn], w_uk[h], preferred_element_type=f32)
                qbuf[:, h, :, 0:dl] = up.astype(bf16).reshape(-1, blk, dl)
                pair = q_rope[:, h // 2 * 128 : h // 2 * 128 + 128]
                if h % 2:
                    pair = jnp.concatenate([pair[:, 64:], pair[:, :64]], axis=1)
                pair = jnp.where(lane < dr, pair, jnp.zeros_like(pair))
                qbuf[:, h, :, dl : dl + 128] = pair.reshape(-1, blk, 128)
        if step == 0:
            own_w.wait()
            for i in (0, 1, 4):
                move_w(i).start()
    for direction in range(2):
        for piece in pieces(direction, 3):
            ring(direction, 3, piece, seen_from(direction, 4)).wait_recv()
    for copy in own:
        copy.wait()
    for rank in range(1, N_DIRECT):
        send(0, rank).wait_recv()
        send(1, rank).wait_recv()


    log2_scale = mscale_sq / math.sqrt(dn + dr) * math.log2(math.e)

    group = 4

    def send_heads(qb, g):
        rows = pl.ds(pl.multiple_of(qb * blk, blk), blk)
        columns = pl.ds(g * group * dv, group * dv)
        return pltpu.make_async_remote_copy(
            src_ref=heads_out.at[0, rows, columns],
            dst_ref=heads_out.at[1, rows, columns],
            send_sem=head_send.at[qb, g],
            recv_sem=head_recv.at[qb, g],
            device_id={"ctx": opposite},
            device_id_type=MESH,
        )

    def attend(qb, carry):
        lane = lax.broadcasted_iota(jnp.int32, (half_blk, 128), 1)
        for j in range(blocks):
            rank, place = picked[qb, j], picked[qb, blocks + j]
            for i in range(block_groups):
                first = j * blk + 16 * i
                kbuf[first : first + 16, 0:dl] = kv[rank, place * block_groups + i]
            pair = rp[rank, place]
            swapped = jnp.concatenate([pair[:, 64:], pair[:, :64]], axis=1)
            zero = jnp.zeros_like(pair)
            kbuf[j * blk : j * blk + half_blk, dl : dl + 128] = jnp.where(lane < dr, pair, zero)
            kbuf[j * blk + half_blk : (j + 1) * blk, dl : dl + 128] = jnp.where(
                lane < dr, swapped, zero
            )
        ahead = lax.broadcasted_iota(jnp.int32, (blk, keys), 1) - picked[qb, 2 * blocks]
        row = lax.broadcasted_iota(jnp.int32, (blk, keys), 0)
        bias = jnp.where((ahead > row) & (ahead < blk), f32(-1e30), f32(0.0))

        key = kbuf[...]
        value = key[:, 0:dl]
        rows = pl.ds(pl.multiple_of(qb * blk, blk), blk)
        all_scores = []
        for g in range(heads // group):
            query = qbuf[qb, g * group : (g + 1) * group].reshape(group * blk, dl + 128)
            all_scores.append(
                lax.dot_general(query, key, (((1,), (1,)), ((), ())), preferred_element_type=f32)
            )
        for g in range(heads // group):
            first = g * group
            scores = all_scores[g]
            scores = (scores.reshape(group, blk, keys) + bias[None]).reshape(group * blk, keys)
            top = jnp.max(scores, axis=1, keepdims=True)
            raised = jnp.exp2((scores - top) * log2_scale)
            total = jnp.sum(raised, axis=1, keepdims=True)
            mixed = jnp.dot(raised.astype(bf16), value, preferred_element_type=f32)
            mixed = (mixed / total).astype(bf16).reshape(group, blk, dl)
            for i in range(group):
                h = first + i
                heads_out[0, rows, h * dv : (h + 1) * dv] = jnp.dot(
                    mixed[i], w_uv[h], preferred_element_type=f32
                ).astype(bf16)
            send_heads(qb, g).start()

        @pl.when(qb == 0)
        def _():
            move_w(0).wait_recv()
            move_w(1).wait_recv()
            for i in (2, 3, 5, 6):
                move_w(i).start()

        return carry

    lax.fori_loop(0, steps, attend, 0)
    move_w(2).wait_recv()
    move_w(3).wait_recv()
    move_w(7).start()
    for i in (4, 5, 6, 7):
        move_w(i).wait_recv()


    def compute(dz, side):
        zz = lax.rem(z + dz, N_Z)
        part[side, zz] = lax.dot_general(
            w_buf[zz], heads_out[side], (((1,), (1,)), ((), ())), preferred_element_type=f32
        )

    def half(direction):
        return slice(direction * half_width, (direction + 1) * half_width)

    def pass_on(direction, step, side):
        return pltpu.make_async_remote_copy(
            src_ref=sent.at[direction, step, side],
            dst_ref=arrived.at[direction, step, side],
            send_sem=sum_send.at[direction, step, side],
            recv_sem=sum_recv.at[direction, step, side],
            device_id={"tp": (right, left)[direction]},
            device_id_type=MESH,
        )

    for step in range(N_Z - 1):
        for side in range(2):
            if step == 0 and side == 1:
                for qb in range(steps):
                    for g in range(heads // group):
                        send_heads(qb, g).wait_recv()
            if step < 3:
                compute(N_Z - 1 - step, side)
                compute(1 + step, side)
            elif step < 5:
                compute((4, 0)[step - 3], side)
            for direction in range(2):
                to = lax.rem(z + (N_Z - 1 - step, 1 + step)[direction], N_Z)
                mine = part[side, to, half(direction), :]
                if step:
                    pass_on(direction, step - 1, side).wait_recv()
                    mine = mine + arrived[direction, step - 1, side].astype(f32)
                sent[direction, step, side] = mine.astype(bf16)
                pass_on(direction, step, side).start()

    def total_of(side, direction):
        return part[side, z, half(direction), :] + arrived[direction, N_Z - 2, side].astype(f32)

    is_home = y_lo == y_hi

    def send_last(side):
        slot = jnp.where(is_home, 0, 1) if side else 0
        return pltpu.make_async_remote_copy(
            src_ref=last_sent.at[side],
            dst_ref=last_got.at[slot],
            send_sem=last_send.at[side],
            recv_sem=last_recv.at[slot],
            device_id={"ctx": opposite if side else me, "tp": home},
            device_id_type=MESH,
        )

    def landed(slot):
        return pltpu.make_async_remote_copy(
            src_ref=last_sent.at[slot],
            dst_ref=last_got.at[slot],
            send_sem=last_send.at[slot],
            recv_sem=last_recv.at[slot],
            device_id={"ctx": opposite, "tp": home},
            device_id_type=MESH,
        )

    for side in (1, 0):
        for direction in range(2):
            pass_on(direction, N_Z - 2, side).wait_recv()
            last_sent[side, half(direction), :] = total_of(side, direction).astype(bf16)
        if side:
            send_last(1).start()

    @pl.when(jnp.logical_not(is_home))
    def _():
        send_last(0).start()
        landed(0).wait_recv()
        landed(1).wait_recv()
        out[...] = (last_got[0].astype(f32) + last_got[1].astype(f32)).astype(bf16)
        send_last(0).wait_send()

    @pl.when(is_home)
    def _():
        landed(0).wait_recv()
        for direction in range(2):
            mine = total_of(0, direction) + last_got[0, half(direction), :].astype(f32)
            out[half(direction), :] = mine.astype(bf16)

    for rank in range(1, N_CTX):
        ask(rank).wait_send()
        send(0, rank).wait_send()
        if rank < N_DIRECT:
            send(1, rank).wait_send()
    send_far_ropes().wait_send()
    for direction in range(2):
        for step in range(4):
            for piece in pieces(direction, step):
                ring(direction, step, piece, seen_from(direction, step)).wait_send()
        for step in range(N_Z - 1):
            for side in range(2):
                pass_on(direction, step, side).wait_send()
    for i in range(8):
        move_w(i).wait_send()
    for qb in range(steps):
        for g in range(heads // group):
            send_heads(qb, g).wait_send()
    send_last(1).wait_send()


def layer(offsets, picked, latent, rope, q_nope, q_rope, w_uk, w_uv, w_out):
    block_groups = latent.shape[1]
    blk = 16 * block_groups
    half, pair = rope.shape[1:]
    queries = q_nope.shape[0]
    heads, dn, dl = w_uk.shape
    dv = w_uv.shape[2]
    steps, blocks = picked.shape[0], picked.shape[1] // 2
    width, depth = w_out.shape
    offsets = jnp.pad(offsets[:, None, :], ((0, 0), (0, 7), (0, 128 - CAP)))
    vmem = pl.BlockSpec(memory_space=pltpu.VMEM)
    smem = pl.BlockSpec(memory_space=pltpu.SMEM)
    dma = pltpu.SemaphoreType.DMA
    sums = (2, N_Z - 1, 2, width // 2, queries)
    return pl.pallas_call(
        layer_kernel,
        out_shape=jax.ShapeDtypeStruct((width, queries), bf16),
        in_specs=[vmem, smem, vmem, vmem] + [pl.BlockSpec(memory_space=pl.ANY)] * 5,
        out_specs=vmem,
        scratch_shapes=[
            pltpu.VMEM(q_nope.shape, bf16),
            pltpu.VMEM(q_rope.shape, bf16),
            pltpu.VMEM(w_uk.shape, bf16),
            pltpu.VMEM(w_uv.shape, bf16),
            dma((4,)),
            pltpu.VMEM(offsets.shape, jnp.int32),
            pltpu.SMEM(offsets.shape, jnp.int32),
            pltpu.VMEM((N_DIRECT, CAP * block_groups, 16, dl), bf16),
            pltpu.VMEM((N_CTX - N_DIRECT, CAP * block_groups // N_Z, 16, dl), bf16),
            pltpu.VMEM((N_DIRECT, CAP, half, pair), bf16),
            pltpu.VMEM((CAP, half, pair), bf16),
            pltpu.VMEM((N_CTX, CAP * block_groups, 16, dl), bf16),
            pltpu.VMEM((N_CTX, CAP, half, pair), bf16),
            dma((N_CTX,)),
            dma((N_CTX,)),
            dma((N_CTX,)),
            dma((3,)),
            dma((2, N_CTX)),
            dma((2, N_CTX)),
            dma((2, 4, 3)),
            dma((2, 4, 3)),
            pltpu.VMEM((steps, heads, blk, dl + 128), bf16),
            pltpu.VMEM((blocks * blk, dl + 128), bf16),
            pltpu.VMEM((2, queries, heads * dv), bf16),
            dma((steps, 2)),
            dma((steps, 2)),
            pltpu.VMEM((N_Z, width, depth), bf16),
            dma((8,)),
            dma((8,)),
            pltpu.VMEM((2, N_Z, width, queries), f32),
            pltpu.VMEM(sums, bf16),
            pltpu.VMEM(sums, bf16),
            dma(sums[:3]),
            dma(sums[:3]),
            pltpu.VMEM((2, width, queries), bf16),
            pltpu.VMEM((2, width, queries), bf16),
            dma((2,)),
            dma((2,)),
        ],
        compiler_params=pltpu.CompilerParams(
            collective_id=2, has_side_effects=True, vmem_limit_bytes=VMEM_LIMIT
        ),
    )(offsets, picked, latent, rope, q_nope, q_rope, w_uk, w_uv, w_out)


def per_device(q_nope, q_rope, latent, key_rope, w_uk, w_uv, w_out, block_lists):
    owners = lax.axis_size("ctx")
    local_heads, head_dim, latent_dim = w_uk.shape
    rope_dim = q_rope.shape[1] // local_heads
    per_owner, row_width = key_rope.shape
    block_len = row_width // rope_dim
    me = lax.axis_index("ctx")
    offsets, ranks, places = slot_tables(block_lists, owners, per_owner, CAP, rank_table(me))
    steps, blocks = block_lists.shape
    own_block = owners * (per_owner - steps) + me * steps + jnp.arange(steps, dtype=jnp.int32)
    is_own = block_lists == own_block[:, None]
    own_at = jnp.sum(
        jnp.where(is_own, (jnp.arange(blocks, dtype=jnp.int32) * block_len + (1 << 20))[None, :], 0), axis=1
    ) - (1 << 20)
    picked = jnp.concatenate([ranks, places, own_at[:, None]], axis=1)
    latent_blocks = latent.reshape(per_owner, block_len // 16, 16, latent_dim)
    rope_pairs = (
        key_rope.reshape(per_owner, 2, block_len // 2, rope_dim)
        .transpose(0, 2, 1, 3)
        .reshape(per_owner, block_len // 2, 2 * rope_dim)
    )
    return layer(
        offsets, picked, latent_blocks, rope_pairs, q_nope, q_rope, w_uk, w_uv, w_out.T
    ).T


def solution(mesh):
    placed = (
        P("ctx", "tp"),
        P("ctx", "tp"),
        P("ctx", None),
        P("ctx", None),
        P("tp", None, None),
        P("tp", None, None),
        P("tp", "ctx"),
        P("ctx", None),
    )
    return jax.shard_map(
        per_device, mesh=mesh, in_specs=placed, out_specs=P("ctx", "tp"), check_vma=False
    )
```

```python
import functools
import math

import jax
import jax.numpy as jnp
from jax import lax
from jax.experimental import pallas as pl
from jax.experimental.pallas import tpu as pltpu
from jax.sharding import PartitionSpec as P

CAP = 6
N_CTX = 16
N_Z = 8
MESH = pl.DeviceIdType.MESH
bf16 = jnp.bfloat16
f32 = jnp.float32
VMEM_LIMIT = 60 * 1024 * 1024

mscale_sq = (0.1 * math.log(40.0) + 1.0) ** 2


RANKS = [(0, 0), (1, 0), (3, 0), (0, 1), (1, 1), (3, 1), (2, 0), (2, 1)]
N_DIRECT = 8


def shifted(me, dx, dy, dk):
    y, x, core = lax.div(me, 8), lax.rem(lax.div(me, 2), 4), lax.rem(me, 2)
    return lax.rem(y + dy, 2) * 8 + lax.rem(x + dx, 4) * 2 + lax.rem(core + dk, 2)


def owner_of(me, rank):
    dx, dy = RANKS[rank // 2]
    return shifted(me, dx, dy, rank % 2)


def asker_of(me, rank):
    dx, dy = RANKS[rank // 2]
    return shifted(me, (4 - dx) % 4, dy, rank % 2)


def rank_of(owner, me):
    dy = ((owner >> 3) - (me >> 3)) & 1
    dx = ((owner >> 1) - (me >> 1)) & 3
    rank = jnp.zeros_like(owner)
    for i, (x, y) in enumerate(RANKS):
        rank = jnp.where((dx == x) & (dy == y), 2 * i, rank)
    return rank + ((owner - me) & 1)


def sum_lanes(values):
    return jnp.sum(values, axis=1, keepdims=True)


def layer_kernel(
    lists,
    latent,
    rope_in,
    q_nope_in,
    q_rope_in,
    w_uk_in,
    w_uv_in,
    w_out,
    out,
    q_nope,
    q_rope,
    w_uk,
    w_uv,
    load_sems,
    rope,
    offsets,
    table,
    picked,
    got,
    asked,
    direct,
    shared,
    ropes,
    far_ropes,
    kv,
    rp,
    ask_send,
    ask_recv,
    ask_local,
    own_sems,
    ctx_send,
    ctx_recv,
    ring_send,
    ring_recv,
    qbuf,
    kbuf,
    heads_out,
    head_send,
    head_recv,
    w_buf,
    w_send,
    w_recv,
    part,
    sent,
    arrived,
    sum_send,
    sum_recv,
    last_sent,
    last_got,
    last_send,
    last_recv,
):
    me = lax.axis_index("ctx")
    t = lax.axis_index("tp")
    z = lax.rem(t, N_Z)
    y_lo = lax.div(t, N_Z)
    y_hi = lax.div(me, 8)
    x_core = lax.rem(me, 8)
    base = t - z
    right = base + lax.rem(z + 1, N_Z)
    left = base + lax.rem(z + N_Z - 1, N_Z)
    opposite = shifted(me, 0, 1, 0)
    other_core = shifted(me, 0, 0, 1)
    x_next = (shifted(me, 1, 0, 0), shifted(me, 3, 0, 0))
    home = y_hi * N_Z + z
    blk = 16 * latent.shape[1]
    half_blk = blk // 2
    block_groups = blk // 16
    share_groups = CAP * block_groups // N_Z
    heads, dn, dl = w_uk.shape
    dv = w_uv.shape[2]
    dr = q_rope.shape[1] // heads
    steps, blocks = lists.shape
    keys = blocks * blk
    queries = q_nope.shape[0]
    width = w_out.shape[0]
    half_width = width // 2

    barrier = pltpu.get_barrier_semaphore()
    for rank in range(1, N_CTX):
        pl.semaphore_signal(
            barrier, inc=1, device_id={"ctx": owner_of(me, rank)}, device_id_type=MESH
        )
    across = lax.rem(t + N_Z, 2 * N_Z)
    for peer in (left, right, across):
        pl.semaphore_signal(barrier, inc=1, device_id={"tp": peer}, device_id_type=MESH)
    pl.semaphore_signal(
        barrier, inc=1, device_id={"ctx": opposite, "tp": across}, device_id_type=MESH
    )

    own_w = pltpu.make_async_copy(w_out, w_buf.at[x_core], own_sems.at[2])
    own_w.start()
    loads = [
        pltpu.make_async_copy(src, dst, load_sems.at[i])
        for i, (src, dst) in enumerate(
            ((q_nope_in, q_nope), (q_rope_in, q_rope), (w_uk_in, w_uk), (w_uv_in, w_uv))
        )
    ]
    for copy in loads:
        copy.start()


    per_owner = latent.shape[0]
    total_blocks = N_CTX * per_owner
    ids = lax.broadcasted_iota(jnp.int32, (8, total_blocks), 1)
    listed = jnp.zeros((8, total_blocks), jnp.int32)
    for qb in range(steps):
        for j in range(blocks):
            listed = jnp.where(ids == lists[qb, j], 1, listed)
    place_of = listed
    shift = 1
    while shift < per_owner:
        moved = pltpu.roll(place_of, shift, 1)
        place_of = place_of + jnp.where((ids & (per_owner - 1)) >= shift, moved, 0)
        shift *= 2
    place_of = place_of - 1

    owner_row = lax.broadcasted_iota(jnp.int32, (N_CTX, total_blocks), 0)
    lane = lax.broadcasted_iota(jnp.int32, (N_CTX, total_blocks), 1)
    here = (owner_row == (lane >> 5)) & (jnp.broadcast_to(listed[0:1], lane.shape) == 1)
    place_row = jnp.broadcast_to(place_of[0:1], lane.shape)
    small_lane = lax.broadcasted_iota(jnp.int32, (N_CTX, 128), 1)
    wanted = jnp.zeros((N_CTX, 128), jnp.int32)
    for s in range(CAP):
        chosen = sum_lanes(jnp.where(here & (place_row == s), lane & (per_owner - 1), 0))
        wanted = jnp.where(small_lane == s, chosen, wanted)
    offsets[:, 0, :] = wanted

    pl.semaphore_wait(barrier, N_CTX + 3)


    def ask(rank):
        return pltpu.make_async_remote_copy(
            src_ref=offsets.at[owner_of(me, rank)],
            dst_ref=got.at[rank],
            send_sem=ask_send.at[rank],
            recv_sem=ask_recv.at[rank],
            device_id={"ctx": owner_of(me, rank)},
            device_id_type=MESH,
        )

    order = list(range(N_DIRECT, N_CTX)) + list(range(1, N_DIRECT))
    for rank in order:
        ask(rank).start()
    got[0] = offsets[me]

    row = lax.broadcasted_iota(jnp.int32, (blocks, total_blocks), 0)
    lane = lax.broadcasted_iota(jnp.int32, (blocks, total_blocks), 1)
    places = jnp.broadcast_to(place_of[0:1], lane.shape)
    small_row = lax.broadcasted_iota(jnp.int32, (blocks, 128), 0)
    small_lane = lax.broadcasted_iota(jnp.int32, (blocks, 128), 1)
    for qb in range(steps):
        block = jnp.zeros((blocks, 128), jnp.int32)
        for j in range(blocks):
            block = jnp.where(small_row == j, lists[qb, j], block)
        place = sum_lanes(jnp.where(lane == block[:, 0:1], places, 0))
        own = block == (total_blocks - N_CTX * steps + me * steps + qb)
        own_at = jnp.max(jnp.where(own, small_row * blk, -(1 << 20)), axis=0, keepdims=True)
        rank = rank_of(block >> 5, me)
        entry = jnp.where(small_lane == 0, rank, jnp.where(small_lane == 1, place, own_at))
        table[qb * blocks : (qb + 1) * blocks, :] = entry
    to_picked = pltpu.make_async_copy(table, picked, load_sems.at[4])
    to_picked.start()

    low = lax.broadcasted_iota(jnp.int32, (per_owner, 128), 1) < dr
    for i in range(half_blk):
        at = i // 2 * 128
        first = rope_in[:, at : at + 128].astype(f32)
        second = rope_in[:, half_blk * dr + at : half_blk * dr + at + 128].astype(f32)
        if i % 2:
            first = pltpu.roll(first, dr, 1)
        else:
            second = pltpu.roll(second, dr, 1)
        rope[:, i, :] = jnp.where(low, first, second)

    def to_scalars(rank):
        return pltpu.make_async_copy(got.at[rank], asked.at[rank], ask_local.at[rank])

    far_dy = jnp.where(lax.div(z, 2) == 2, 0, 1)
    far_dx = jnp.where(z < 4, 1 + 2 * lax.div(z, 2), 2)
    far_asker = shifted(me, lax.rem(4 - far_dx, 4), far_dy, lax.rem(z, 2))

    def send(kind, rank):
        if rank >= N_DIRECT:
            src = shared.at[rank - N_DIRECT]
            dst = kv.at[rank, pl.ds(z * share_groups, share_groups)]
        else:
            src, dst = ((direct.at[rank], kv.at[rank]), (ropes.at[rank], rp.at[rank]))[kind]
        return pltpu.make_async_remote_copy(
            src_ref=src,
            dst_ref=dst,
            send_sem=ctx_send.at[kind, rank],
            recv_sem=ctx_recv.at[kind, rank],
            device_id={"ctx": asker_of(me, rank)},
            device_id_type=MESH,
        )

    def send_far_ropes():
        return pltpu.make_async_remote_copy(
            src_ref=far_ropes,
            dst_ref=rp.at[N_DIRECT + z],
            send_sem=ctx_send.at[1, N_DIRECT],
            recv_sem=ctx_recv.at[1, N_DIRECT],
            device_id={"ctx": far_asker},
            device_id_type=MESH,
        )

    for rank in order:
        ask(rank).wait_recv()
        to_scalars(rank).start()
    to_scalars(0).start()
    for rank in range(N_DIRECT, N_CTX):
        to_scalars(rank).wait()
        for i in range(share_groups):
            group = z * share_groups + i
            block = asked[rank, 0, lax.div(group, block_groups)]
            shared[rank - N_DIRECT, i] = latent[block, lax.rem(group, block_groups)]
        send(0, rank).start()
    for s in range(CAP):
        far_ropes[s] = rope[asked[N_DIRECT + z, 0, s]].astype(bf16)
    send_far_ropes().start()
    for rank in list(range(1, N_DIRECT)) + [0]:
        to_scalars(rank).wait()
        for s in range(CAP):
            block = asked[rank, 0, s]
            direct[rank, s * block_groups : (s + 1) * block_groups] = latent[block]
            ropes[rank, s] = rope[block].astype(bf16)
        if rank:
            send(0, rank).start()
            send(1, rank).start()
    own = [
        pltpu.make_async_copy(direct.at[0], kv.at[0], own_sems.at[0]),
        pltpu.make_async_copy(ropes.at[0], rp.at[0], own_sems.at[1]),
    ]
    for copy in own:
        copy.start()


    def ring(direction, step, piece, zz):
        if piece == 2:
            moved = rp.at[N_DIRECT + zz]
        else:
            moved = kv.at[pl.ds(N_DIRECT + 4 * piece, 4), pl.ds(zz * share_groups, share_groups)]
        return pltpu.make_async_remote_copy(
            src_ref=moved,
            dst_ref=moved,
            send_sem=ring_send.at[direction, step, piece],
            recv_sem=ring_recv.at[direction, step, piece],
            device_id={"tp": (right, left)[direction]},
            device_id_type=MESH,
        )

    def pieces(direction, step):
        return (0, 1, 2) if step < 3 else ((0,), (1, 2))[direction]

    def seen_from(direction, step):
        return lax.rem(z + (N_Z - step if direction == 0 else step), N_Z)


    def column(dx):
        return lax.rem(x_core + 2 * dx, 8)

    def move_w(i):
        source = (0, 0, 3, 1, 0, 3, 1, 2)[i]
        rows = pl.ds((i - 2) * half_width, half_width) if i in (2, 3) else pl.ds(0, width)
        peer = other_core if i >= 4 else x_next[i % 2]
        block = w_buf.at[column(source), rows]
        return pltpu.make_async_remote_copy(
            src_ref=block,
            dst_ref=block,
            send_sem=w_send.at[i],
            recv_sem=w_recv.at[i],
            device_id={"ctx": peer},
            device_id_type=MESH,
        )

    for step in range(4):
        for piece in range(3):
            if step == 0:
                if piece == 2:
                    send_far_ropes().wait_recv()
                else:
                    for rank in range(N_DIRECT + 4 * piece, N_DIRECT + 4 * piece + 4):
                        send(0, rank).wait_recv()
            for direction in range(2):
                if step:
                    ring(direction, step - 1, piece, seen_from(direction, step)).wait_recv()
                if piece in pieces(direction, step):
                    ring(direction, step, piece, seen_from(direction, step)).start()
        if step == 0:
            for copy in loads:
                copy.wait()
            lane = lax.broadcasted_iota(jnp.int32, (queries, 128), 1)
            for h in range(heads):
                up = jnp.dot(q_nope[:, h * dn : (h + 1) * dn], w_uk[h], preferred_element_type=f32)
                qbuf[:, h, :, 0:dl] = up.astype(bf16).reshape(-1, blk, dl)
                pair = q_rope[:, h // 2 * 128 : h // 2 * 128 + 128]
                if h % 2:
                    pair = jnp.concatenate([pair[:, 64:], pair[:, :64]], axis=1)
                pair = jnp.where(lane < dr, pair, jnp.zeros_like(pair))
                qbuf[:, h, :, dl : dl + 128] = pair.reshape(-1, blk, 128)
        if step == 0:
            own_w.wait()
            for i in (0, 1, 4):
                move_w(i).start()
    for direction in range(2):
        for piece in pieces(direction, 3):
            ring(direction, 3, piece, seen_from(direction, 4)).wait_recv()
    for copy in own:
        copy.wait()
    for rank in range(1, N_DIRECT):
        send(0, rank).wait_recv()
        send(1, rank).wait_recv()


    log2_scale = mscale_sq / math.sqrt(dn + dr) * math.log2(math.e)

    group = 4

    def send_heads(qb, g):
        rows = pl.ds(pl.multiple_of(qb * blk, blk), blk)
        columns = pl.ds(g * group * dv, group * dv)
        return pltpu.make_async_remote_copy(
            src_ref=heads_out.at[0, rows, columns],
            dst_ref=heads_out.at[1, rows, columns],
            send_sem=head_send.at[qb, g],
            recv_sem=head_recv.at[qb, g],
            device_id={"ctx": opposite},
            device_id_type=MESH,
        )

    def attend(qb, carry):
        lane = lax.broadcasted_iota(jnp.int32, (half_blk, 128), 1)
        for j in range(blocks):
            rank, place = picked[qb * blocks + j, 0], picked[qb * blocks + j, 1]
            for i in range(block_groups):
                first = j * blk + 16 * i
                kbuf[first : first + 16, 0:dl] = kv[rank, place * block_groups + i]
            pair = rp[rank, place]
            swapped = jnp.concatenate([pair[:, 64:], pair[:, :64]], axis=1)
            zero = jnp.zeros_like(pair)
            kbuf[j * blk : j * blk + half_blk, dl : dl + 128] = jnp.where(lane < dr, pair, zero)
            kbuf[j * blk + half_blk : (j + 1) * blk, dl : dl + 128] = jnp.where(
                lane < dr, swapped, zero
            )
        ahead = lax.broadcasted_iota(jnp.int32, (blk, keys), 1) - picked[qb * blocks, 2]
        row = lax.broadcasted_iota(jnp.int32, (blk, keys), 0)
        bias = jnp.where((ahead > row) & (ahead < blk), f32(-1e30), f32(0.0))

        key = kbuf[...]
        value = key[:, 0:dl]
        rows = pl.ds(pl.multiple_of(qb * blk, blk), blk)
        all_scores = []
        for g in range(heads // group):
            query = qbuf[qb, g * group : (g + 1) * group].reshape(group * blk, dl + 128)
            all_scores.append(
                lax.dot_general(query, key, (((1,), (1,)), ((), ())), preferred_element_type=f32)
            )
        for g in range(heads // group):
            first = g * group
            scores = all_scores[g]
            scores = (scores.reshape(group, blk, keys) + bias[None]).reshape(group * blk, keys)
            top = jnp.max(scores, axis=1, keepdims=True)
            raised = jnp.exp2((scores - top) * log2_scale)
            total = jnp.sum(raised, axis=1, keepdims=True)
            mixed = jnp.dot(raised.astype(bf16), value, preferred_element_type=f32)
            mixed = (mixed / total).astype(bf16).reshape(group, blk, dl)
            for i in range(group):
                h = first + i
                heads_out[0, rows, h * dv : (h + 1) * dv] = jnp.dot(
                    mixed[i], w_uv[h], preferred_element_type=f32
                ).astype(bf16)
            send_heads(qb, g).start()

        @pl.when(qb == 0)
        def _():
            move_w(0).wait_recv()
            move_w(1).wait_recv()
            for i in (2, 3, 5, 6):
                move_w(i).start()

        return carry

    to_picked.wait()
    lax.fori_loop(0, steps, attend, 0)
    move_w(2).wait_recv()
    move_w(3).wait_recv()
    move_w(7).start()
    for i in (4, 5, 6, 7):
        move_w(i).wait_recv()


    def compute(dz, side):
        zz = lax.rem(z + dz, N_Z)
        part[side, zz] = lax.dot_general(
            w_buf[zz], heads_out[side], (((1,), (1,)), ((), ())), preferred_element_type=f32
        )

    def half(direction):
        return slice(direction * half_width, (direction + 1) * half_width)

    def pass_on(direction, step, side):
        return pltpu.make_async_remote_copy(
            src_ref=sent.at[direction, step, side],
            dst_ref=arrived.at[direction, step, side],
            send_sem=sum_send.at[direction, step, side],
            recv_sem=sum_recv.at[direction, step, side],
            device_id={"tp": (right, left)[direction]},
            device_id_type=MESH,
        )

    for step in range(N_Z - 1):
        for side in range(2):
            if step == 0 and side == 1:
                for qb in range(steps):
                    for g in range(heads // group):
                        send_heads(qb, g).wait_recv()
            if step < 3:
                compute(N_Z - 1 - step, side)
                compute(1 + step, side)
            elif step < 5:
                compute((4, 0)[step - 3], side)
            for direction in range(2):
                to = lax.rem(z + (N_Z - 1 - step, 1 + step)[direction], N_Z)
                mine = part[side, to, half(direction), :]
                if step:
                    pass_on(direction, step - 1, side).wait_recv()
                    mine = mine + arrived[direction, step - 1, side].astype(f32)
                sent[direction, step, side] = mine.astype(bf16)
                pass_on(direction, step, side).start()

    def total_of(side, direction):
        return part[side, z, half(direction), :] + arrived[direction, N_Z - 2, side].astype(f32)

    is_home = y_lo == y_hi

    def send_last(side, direction):
        slot = jnp.where(is_home, 0, 1) if side else 0
        return pltpu.make_async_remote_copy(
            src_ref=last_sent.at[side, direction],
            dst_ref=last_got.at[slot, direction],
            send_sem=last_send.at[side, direction],
            recv_sem=last_recv.at[slot, direction],
            device_id={"ctx": opposite if side else me, "tp": home},
            device_id_type=MESH,
        )

    def landed(slot, direction):
        return pltpu.make_async_remote_copy(
            src_ref=last_sent.at[slot, direction],
            dst_ref=last_got.at[slot, direction],
            send_sem=last_send.at[slot, direction],
            recv_sem=last_recv.at[slot, direction],
            device_id={"ctx": opposite, "tp": home},
            device_id_type=MESH,
        )

    for direction in range(2):
        pass_on(direction, N_Z - 2, 0).wait_recv()
        last_sent[0, direction] = total_of(0, direction).astype(bf16)

        @pl.when(jnp.logical_not(is_home))
        def _():
            send_last(0, direction).start()

    for direction in range(2):
        pass_on(direction, N_Z - 2, 1).wait_recv()
        last_sent[1, direction] = total_of(1, direction).astype(bf16)
        send_last(1, direction).start()

    @pl.when(jnp.logical_not(is_home))
    def _():
        for direction in range(2):
            landed(0, direction).wait_recv()
            landed(1, direction).wait_recv()
            sum_of_both = last_got[0, direction].astype(f32) + last_got[1, direction].astype(f32)
            out[half(direction), :] = sum_of_both.astype(bf16)
            send_last(0, direction).wait_send()

    @pl.when(is_home)
    def _():
        for direction in range(2):
            landed(0, direction).wait_recv()
            mine = total_of(0, direction) + last_got[0, direction].astype(f32)
            out[half(direction), :] = mine.astype(bf16)

    for rank in range(1, N_CTX):
        ask(rank).wait_send()
        send(0, rank).wait_send()
        if rank < N_DIRECT:
            send(1, rank).wait_send()
    send_far_ropes().wait_send()
    for direction in range(2):
        for step in range(4):
            for piece in pieces(direction, step):
                ring(direction, step, piece, seen_from(direction, step)).wait_send()
        for step in range(N_Z - 1):
            for side in range(2):
                pass_on(direction, step, side).wait_send()
    for i in range(8):
        move_w(i).wait_send()
    for qb in range(steps):
        for g in range(heads // group):
            send_heads(qb, g).wait_send()
    for direction in range(2):
        send_last(1, direction).wait_send()


def layer(lists, latent, rope, q_nope, q_rope, w_uk, w_uv, w_out):
    block_groups = latent.shape[1]
    blk = 16 * block_groups
    half, pair = blk // 2, 2 * rope.shape[1] // blk
    queries = q_nope.shape[0]
    heads, dn, dl = w_uk.shape
    dv = w_uv.shape[2]
    steps, blocks = lists.shape
    width, depth = w_out.shape
    asks = (N_CTX, 8, 128)
    vmem = pl.BlockSpec(memory_space=pltpu.VMEM)
    smem = pl.BlockSpec(memory_space=pltpu.SMEM)
    dma = pltpu.SemaphoreType.DMA
    sums = (2, N_Z - 1, 2, width // 2, queries)
    return pl.pallas_call(
        layer_kernel,
        out_shape=jax.ShapeDtypeStruct((width, queries), bf16),
        in_specs=[smem, vmem, vmem] + [pl.BlockSpec(memory_space=pl.ANY)] * 5,
        out_specs=vmem,
        scratch_shapes=[
            pltpu.VMEM(q_nope.shape, bf16),
            pltpu.VMEM(q_rope.shape, bf16),
            pltpu.VMEM(w_uk.shape, bf16),
            pltpu.VMEM(w_uv.shape, bf16),
            dma((5,)),
            pltpu.VMEM((latent.shape[0], half, pair), f32),
            pltpu.VMEM(asks, jnp.int32),
            pltpu.VMEM((steps * blocks, 128), jnp.int32),
            pltpu.SMEM((steps * blocks, 128), jnp.int32),
            pltpu.VMEM(asks, jnp.int32),
            pltpu.SMEM(asks, jnp.int32),
            pltpu.VMEM((N_DIRECT, CAP * block_groups, 16, dl), bf16),
            pltpu.VMEM((N_CTX - N_DIRECT, CAP * block_groups // N_Z, 16, dl), bf16),
            pltpu.VMEM((N_DIRECT, CAP, half, pair), bf16),
            pltpu.VMEM((CAP, half, pair), bf16),
            pltpu.VMEM((N_CTX, CAP * block_groups, 16, dl), bf16),
            pltpu.VMEM((N_CTX, CAP, half, pair), bf16),
            dma((N_CTX,)),
            dma((N_CTX,)),
            dma((N_CTX,)),
            dma((3,)),
            dma((2, N_CTX)),
            dma((2, N_CTX)),
            dma((2, 4, 3)),
            dma((2, 4, 3)),
            pltpu.VMEM((steps, heads, blk, dl + 128), bf16),
            pltpu.VMEM((blocks * blk, dl + 128), bf16),
            pltpu.VMEM((2, queries, heads * dv), bf16),
            dma((steps, 2)),
            dma((steps, 2)),
            pltpu.VMEM((N_Z, width, depth), bf16),
            dma((8,)),
            dma((8,)),
            pltpu.VMEM((2, N_Z, width, queries), f32),
            pltpu.VMEM(sums, bf16),
            pltpu.VMEM(sums, bf16),
            dma(sums[:3]),
            dma(sums[:3]),
            pltpu.VMEM((2, 2, width // 2, queries), bf16),
            pltpu.VMEM((2, 2, width // 2, queries), bf16),
            dma((2, 2)),
            dma((2, 2)),
        ],
        compiler_params=pltpu.CompilerParams(
            collective_id=2, has_side_effects=True, vmem_limit_bytes=VMEM_LIMIT
        ),
    )(lists, latent, rope, q_nope, q_rope, w_uk, w_uv, w_out)


def per_device(q_nope, q_rope, latent, key_rope, w_uk, w_uv, w_out, block_lists):
    per_owner = key_rope.shape[0]
    latent_blocks = latent.reshape(per_owner, -1, 16, latent.shape[1])
    return layer(
        block_lists, latent_blocks, key_rope, q_nope, q_rope, w_uk, w_uv, w_out.T
    ).T


def solution(mesh):
    placed = (
        P("ctx", "tp"),
        P("ctx", "tp"),
        P("ctx", None),
        P("ctx", None),
        P("tp", None, None),
        P("tp", None, None),
        P("tp", "ctx"),
        P("ctx", None),
    )
    return jax.shard_map(
        per_device, mesh=mesh, in_specs=placed, out_specs=P("ctx", "tp"), check_vma=False
    )
```

```python
import functools
import math

import jax
import jax.numpy as jnp
from jax import lax
from jax.experimental import pallas as pl
from jax.experimental.pallas import tpu as pltpu
from jax.sharding import PartitionSpec as P

CAP = 6
N_CTX = 16
N_Z = 8
MESH = pl.DeviceIdType.MESH
bf16 = jnp.bfloat16
f32 = jnp.float32
VMEM_LIMIT = 60 * 1024 * 1024

mscale_sq = (0.1 * math.log(40.0) + 1.0) ** 2


RANKS = [(0, 0), (1, 0), (3, 0), (0, 1), (1, 1), (3, 1), (2, 0), (2, 1)]
N_DIRECT = 8


def shifted(me, dx, dy, dk):
    y, x, core = lax.div(me, 8), lax.rem(lax.div(me, 2), 4), lax.rem(me, 2)
    return lax.rem(y + dy, 2) * 8 + lax.rem(x + dx, 4) * 2 + lax.rem(core + dk, 2)


def owner_of(me, rank):
    dx, dy = RANKS[rank // 2]
    return shifted(me, dx, dy, rank % 2)


def asker_of(me, rank):
    dx, dy = RANKS[rank // 2]
    return shifted(me, (4 - dx) % 4, dy, rank % 2)


def rank_of(owner, me):
    dy = ((owner >> 3) - (me >> 3)) & 1
    dx = ((owner >> 1) - (me >> 1)) & 3
    rank = jnp.zeros_like(owner)
    for i, (x, y) in enumerate(RANKS):
        rank = jnp.where((dx == x) & (dy == y), 2 * i, rank)
    return rank + ((owner - me) & 1)


def sum_lanes(values):
    return jnp.sum(values, axis=1, keepdims=True)


def layer_kernel(
    lists,
    latent,
    rope_in,
    q_nope_in,
    q_rope_in,
    w_uk_in,
    w_uv_in,
    w_out,
    out,
    q_nope,
    q_rope,
    w_uk,
    w_uv,
    load_sems,
    rope,
    offsets,
    table,
    picked,
    got,
    asked,
    direct,
    shared,
    ropes,
    far_ropes,
    kv,
    rp,
    ask_send,
    ask_recv,
    ask_local,
    own_sems,
    ctx_send,
    ctx_recv,
    ring_send,
    ring_recv,
    qbuf,
    kbuf,
    heads_out,
    head_send,
    head_recv,
    w_buf,
    w_send,
    w_recv,
    part,
    sent,
    arrived,
    sum_send,
    sum_recv,
    last_sent,
    last_got,
    last_send,
    last_recv,
):
    me = lax.axis_index("ctx")
    t = lax.axis_index("tp")
    z = lax.rem(t, N_Z)
    y_lo = lax.div(t, N_Z)
    y_hi = lax.div(me, 8)
    x_core = lax.rem(me, 8)
    base = t - z
    right = base + lax.rem(z + 1, N_Z)
    left = base + lax.rem(z + N_Z - 1, N_Z)
    opposite = shifted(me, 0, 1, 0)
    other_core = shifted(me, 0, 0, 1)
    x_next = (shifted(me, 1, 0, 0), shifted(me, 3, 0, 0))
    home = y_hi * N_Z + z
    blk = 16 * latent.shape[1]
    half_blk = blk // 2
    block_groups = blk // 16
    share_groups = CAP * block_groups // N_Z
    heads, dn, dl = w_uk.shape
    dv = w_uv.shape[2]
    dr = q_rope.shape[1] // heads
    steps, blocks = lists.shape
    keys = blocks * blk
    queries = q_nope.shape[0]
    width = w_out.shape[0]
    half_width = width // 2

    barrier = pltpu.get_barrier_semaphore()
    for rank in range(1, N_CTX):
        pl.semaphore_signal(
            barrier, inc=1, device_id={"ctx": owner_of(me, rank)}, device_id_type=MESH
        )
    across = lax.rem(t + N_Z, 2 * N_Z)
    for peer in (left, right, across):
        pl.semaphore_signal(barrier, inc=1, device_id={"tp": peer}, device_id_type=MESH)
    pl.semaphore_signal(
        barrier, inc=1, device_id={"ctx": opposite, "tp": across}, device_id_type=MESH
    )

    own_w = pltpu.make_async_copy(w_out, w_buf.at[x_core], own_sems.at[2])
    own_w.start()
    loads = [
        pltpu.make_async_copy(src, dst, load_sems.at[i])
        for i, (src, dst) in enumerate(
            ((q_nope_in, q_nope), (q_rope_in, q_rope), (w_uk_in, w_uk), (w_uv_in, w_uv))
        )
    ]
    for copy in loads:
        copy.start()


    per_owner = latent.shape[0]
    total_blocks = N_CTX * per_owner
    ids = lax.broadcasted_iota(jnp.int32, (8, total_blocks), 1)
    listed = jnp.zeros((8, total_blocks), jnp.int32)
    for qb in range(steps):
        for j in range(blocks):
            listed = jnp.where(ids == lists[qb, j], 1, listed)
    place_of = listed
    shift = 1
    while shift < per_owner:
        moved = pltpu.roll(place_of, shift, 1)
        place_of = place_of + jnp.where((ids & (per_owner - 1)) >= shift, moved, 0)
        shift *= 2
    place_of = place_of - 1

    owner_row = lax.broadcasted_iota(jnp.int32, (N_CTX, total_blocks), 0)
    lane = lax.broadcasted_iota(jnp.int32, (N_CTX, total_blocks), 1)
    here = (owner_row == (lane >> 5)) & (jnp.broadcast_to(listed[0:1], lane.shape) == 1)
    place_row = jnp.broadcast_to(place_of[0:1], lane.shape)
    small_lane = lax.broadcasted_iota(jnp.int32, (N_CTX, 128), 1)
    wanted = jnp.zeros((N_CTX, 128), jnp.int32)
    for s in range(CAP):
        chosen = sum_lanes(jnp.where(here & (place_row == s), lane & (per_owner - 1), 0))
        wanted = jnp.where(small_lane == s, chosen, wanted)
    offsets[:, 0, :] = wanted

    pl.semaphore_wait(barrier, N_CTX + 3)


    def ask(rank):
        return pltpu.make_async_remote_copy(
            src_ref=offsets.at[owner_of(me, rank)],
            dst_ref=got.at[rank],
            send_sem=ask_send.at[rank],
            recv_sem=ask_recv.at[rank],
            device_id={"ctx": owner_of(me, rank)},
            device_id_type=MESH,
        )

    order = list(range(N_DIRECT, N_CTX)) + list(range(1, N_DIRECT))
    for rank in order:
        ask(rank).start()
    got[0] = offsets[me]

    row = lax.broadcasted_iota(jnp.int32, (blocks, total_blocks), 0)
    lane = lax.broadcasted_iota(jnp.int32, (blocks, total_blocks), 1)
    places = jnp.broadcast_to(place_of[0:1], lane.shape)
    small_row = lax.broadcasted_iota(jnp.int32, (blocks, 128), 0)
    small_lane = lax.broadcasted_iota(jnp.int32, (blocks, 128), 1)
    for qb in range(steps):
        block = jnp.zeros((blocks, 128), jnp.int32)
        for j in range(blocks):
            block = jnp.where(small_row == j, lists[qb, j], block)
        place = sum_lanes(jnp.where(lane == block[:, 0:1], places, 0))
        own = block == (total_blocks - N_CTX * steps + me * steps + qb)
        own_at = jnp.max(jnp.where(own, small_row * blk, -(1 << 20)), axis=0, keepdims=True)
        rank = rank_of(block >> 5, me)
        entry = jnp.where(small_lane == 0, rank, jnp.where(small_lane == 1, place, own_at))
        table[qb * blocks : (qb + 1) * blocks, :] = entry
    to_picked = pltpu.make_async_copy(table, picked, load_sems.at[4])
    to_picked.start()

    low = lax.broadcasted_iota(jnp.int32, (per_owner, 128), 1) < dr
    for i in range(half_blk):
        at = i // 2 * 128
        first = rope_in[:, at : at + 128].astype(f32)
        second = rope_in[:, half_blk * dr + at : half_blk * dr + at + 128].astype(f32)
        if i % 2:
            first = pltpu.roll(first, dr, 1)
        else:
            second = pltpu.roll(second, dr, 1)
        rope[:, i, :] = jnp.where(low, first, second)

    def to_scalars(rank):
        return pltpu.make_async_copy(got.at[rank], asked.at[rank], ask_local.at[rank])

    far_dy = jnp.where(lax.div(z, 2) == 2, 0, 1)
    far_dx = jnp.where(z < 4, 1 + 2 * lax.div(z, 2), 2)
    far_asker = shifted(me, lax.rem(4 - far_dx, 4), far_dy, lax.rem(z, 2))

    first_far = N_DIRECT + 4 * y_lo

    def far_asker_of(i):
        dx = jnp.where(y_lo == 0, 1 + 2 * (i // 2), 2)
        dy = jnp.where(y_lo == 0, 1, i // 2)
        return shifted(me, lax.rem(4 - dx, 4), dy, i % 2)

    def swap_far():
        moved = kv.at[pl.ds(first_far, 4), pl.ds(z * share_groups, share_groups)]
        return pltpu.make_async_remote_copy(
            src_ref=moved,
            dst_ref=moved,
            send_sem=ctx_send.at[1, N_DIRECT + 1],
            recv_sem=ctx_recv.at[1, N_DIRECT + 1],
            device_id={"tp": across},
            device_id_type=MESH,
        )

    def send(kind, rank):
        if rank >= N_DIRECT:
            src = shared.at[rank - N_DIRECT]
            dst = kv.at[first_far + rank - N_DIRECT, pl.ds(z * share_groups, share_groups)]
        else:
            src, dst = ((direct.at[rank], kv.at[rank]), (ropes.at[rank], rp.at[rank]))[kind]
        return pltpu.make_async_remote_copy(
            src_ref=src,
            dst_ref=dst,
            send_sem=ctx_send.at[kind, rank],
            recv_sem=ctx_recv.at[kind, rank],
            device_id={"ctx": far_asker_of(rank - N_DIRECT) if rank >= N_DIRECT else asker_of(me, rank)},
            device_id_type=MESH,
        )

    def send_far_ropes():
        return pltpu.make_async_remote_copy(
            src_ref=far_ropes,
            dst_ref=rp.at[N_DIRECT + z],
            send_sem=ctx_send.at[1, N_DIRECT],
            recv_sem=ctx_recv.at[1, N_DIRECT],
            device_id={"ctx": far_asker},
            device_id_type=MESH,
        )

    for rank in order:
        ask(rank).wait_recv()
        to_scalars(rank).start()
    to_scalars(0).start()
    for rank in range(N_DIRECT, N_CTX):
        to_scalars(rank).wait()
    for rank in range(N_DIRECT, N_DIRECT + 4):
        for i in range(share_groups):
            group = z * share_groups + i
            block = asked[first_far + rank - N_DIRECT, 0, lax.div(group, block_groups)]
            shared[rank - N_DIRECT, i] = latent[block, lax.rem(group, block_groups)]
        send(0, rank).start()
    for s in range(CAP):
        far_ropes[s] = rope[asked[N_DIRECT + z, 0, s]].astype(bf16)
    send_far_ropes().start()
    for rank in list(range(1, N_DIRECT)) + [0]:
        to_scalars(rank).wait()
        for s in range(CAP):
            block = asked[rank, 0, s]
            direct[rank, s * block_groups : (s + 1) * block_groups] = latent[block]
            ropes[rank, s] = rope[block].astype(bf16)
        if rank:
            send(0, rank).start()
            send(1, rank).start()
    own = [
        pltpu.make_async_copy(direct.at[0], kv.at[0], own_sems.at[0]),
        pltpu.make_async_copy(ropes.at[0], rp.at[0], own_sems.at[1]),
    ]
    for copy in own:
        copy.start()


    def ring(direction, step, piece, zz):
        if piece == 2:
            moved = rp.at[N_DIRECT + zz]
        else:
            fetched_by = y_lo if piece == 0 else 1 - y_lo
            moved = kv.at[pl.ds(N_DIRECT + 4 * fetched_by, 4), pl.ds(zz * share_groups, share_groups)]
        return pltpu.make_async_remote_copy(
            src_ref=moved,
            dst_ref=moved,
            send_sem=ring_send.at[direction, step, piece],
            recv_sem=ring_recv.at[direction, step, piece],
            device_id={"tp": (right, left)[direction]},
            device_id_type=MESH,
        )

    def pieces(direction, step):
        return (0, 1, 2) if step < 3 else ((0,), (1, 2))[direction]

    def seen_from(direction, step):
        return lax.rem(z + (N_Z - step if direction == 0 else step), N_Z)


    def column(dx):
        return lax.rem(x_core + 2 * dx, 8)

    def move_w(i):
        source = (0, 0, 3, 1, 0, 3, 1, 2)[i]
        rows = pl.ds((i - 2) * half_width, half_width) if i in (2, 3) else pl.ds(0, width)
        peer = other_core if i >= 4 else x_next[i % 2]
        block = w_buf.at[column(source), rows]
        return pltpu.make_async_remote_copy(
            src_ref=block,
            dst_ref=block,
            send_sem=w_send.at[i],
            recv_sem=w_recv.at[i],
            device_id={"ctx": peer},
            device_id_type=MESH,
        )

    for step in range(4):
        for piece in (0, 2, 1):
            if step == 0:
                if piece == 2:
                    send_far_ropes().wait_recv()
                elif piece == 1:
                    swap_far().wait_recv()
                else:
                    for rank in range(N_DIRECT, N_DIRECT + 4):
                        send(0, rank).wait_recv()
                    swap_far().start()
            for direction in range(2):
                if step:
                    ring(direction, step - 1, piece, seen_from(direction, step)).wait_recv()
                if piece in pieces(direction, step):
                    ring(direction, step, piece, seen_from(direction, step)).start()
        if step == 0:
            for copy in loads:
                copy.wait()
            lane = lax.broadcasted_iota(jnp.int32, (queries, 128), 1)
            for h in range(heads):
                up = jnp.dot(q_nope[:, h * dn : (h + 1) * dn], w_uk[h], preferred_element_type=f32)
                qbuf[:, h, :, 0:dl] = up.astype(bf16).reshape(-1, blk, dl)
                pair = q_rope[:, h // 2 * 128 : h // 2 * 128 + 128]
                if h % 2:
                    pair = jnp.concatenate([pair[:, 64:], pair[:, :64]], axis=1)
                pair = jnp.where(lane < dr, pair, jnp.zeros_like(pair))
                qbuf[:, h, :, dl : dl + 128] = pair.reshape(-1, blk, 128)
        if step == 0:
            own_w.wait()
            for i in (0, 1, 4):
                move_w(i).start()
    for direction in range(2):
        for piece in pieces(direction, 3):
            ring(direction, 3, piece, seen_from(direction, 4)).wait_recv()
    for copy in own:
        copy.wait()
    for rank in range(1, N_DIRECT):
        send(0, rank).wait_recv()
        send(1, rank).wait_recv()


    log2_scale = mscale_sq / math.sqrt(dn + dr) * math.log2(math.e)

    group = 4

    def send_heads(qb, g):
        rows = pl.ds(pl.multiple_of(qb * blk, blk), blk)
        columns = pl.ds(g * group * dv, group * dv)
        return pltpu.make_async_remote_copy(
            src_ref=heads_out.at[0, rows, columns],
            dst_ref=heads_out.at[1, rows, columns],
            send_sem=head_send.at[qb, g],
            recv_sem=head_recv.at[qb, g],
            device_id={"ctx": opposite},
            device_id_type=MESH,
        )

    def attend(qb, carry):
        lane = lax.broadcasted_iota(jnp.int32, (half_blk, 128), 1)
        for j in range(blocks):
            rank, place = picked[qb * blocks + j, 0], picked[qb * blocks + j, 1]
            for i in range(block_groups):
                first = j * blk + 16 * i
                kbuf[first : first + 16, 0:dl] = kv[rank, place * block_groups + i]
            pair = rp[rank, place]
            swapped = jnp.concatenate([pair[:, 64:], pair[:, :64]], axis=1)
            zero = jnp.zeros_like(pair)
            kbuf[j * blk : j * blk + half_blk, dl : dl + 128] = jnp.where(lane < dr, pair, zero)
            kbuf[j * blk + half_blk : (j + 1) * blk, dl : dl + 128] = jnp.where(
                lane < dr, swapped, zero
            )
        ahead = lax.broadcasted_iota(jnp.int32, (blk, keys), 1) - picked[qb * blocks, 2]
        row = lax.broadcasted_iota(jnp.int32, (blk, keys), 0)
        bias = jnp.where((ahead > row) & (ahead < blk), f32(-1e30), f32(0.0))

        key = kbuf[...]
        value = key[:, 0:dl]
        rows = pl.ds(pl.multiple_of(qb * blk, blk), blk)
        all_scores = []
        for g in range(heads // group):
            query = qbuf[qb, g * group : (g + 1) * group].reshape(group * blk, dl + 128)
            all_scores.append(
                lax.dot_general(query, key, (((1,), (1,)), ((), ())), preferred_element_type=f32)
            )
        for g in range(heads // group):
            first = g * group
            scores = all_scores[g]
            scores = (scores.reshape(group, blk, keys) + bias[None]).reshape(group * blk, keys)
            top = jnp.max(scores, axis=1, keepdims=True)
            raised = jnp.exp2((scores - top) * log2_scale)
            total = jnp.sum(raised, axis=1, keepdims=True)
            mixed = jnp.dot(raised.astype(bf16), value, preferred_element_type=f32)
            mixed = (mixed / total).astype(bf16).reshape(group, blk, dl)
            for i in range(group):
                h = first + i
                heads_out[0, rows, h * dv : (h + 1) * dv] = jnp.dot(
                    mixed[i], w_uv[h], preferred_element_type=f32
                ).astype(bf16)
            send_heads(qb, g).start()

        @pl.when(qb == 0)
        def _():
            move_w(0).wait_recv()
            move_w(1).wait_recv()
            for i in (2, 3, 5, 6):
                move_w(i).start()

        return carry

    to_picked.wait()
    lax.fori_loop(0, steps, attend, 0)
    move_w(2).wait_recv()
    move_w(3).wait_recv()
    move_w(7).start()
    for i in (4, 5, 6, 7):
        move_w(i).wait_recv()


    def compute(dz, side):
        zz = lax.rem(z + dz, N_Z)
        part[side, zz] = lax.dot_general(
            w_buf[zz], heads_out[side], (((1,), (1,)), ((), ())), preferred_element_type=f32
        )

    def half(direction):
        return slice(direction * half_width, (direction + 1) * half_width)

    def pass_on(direction, step, side):
        return pltpu.make_async_remote_copy(
            src_ref=sent.at[direction, step, side],
            dst_ref=arrived.at[direction, step, side],
            send_sem=sum_send.at[direction, step, side],
            recv_sem=sum_recv.at[direction, step, side],
            device_id={"tp": (right, left)[direction]},
            device_id_type=MESH,
        )

    for step in range(N_Z - 1):
        for side in range(2):
            if step == 0 and side == 1:
                for qb in range(steps):
                    for g in range(heads // group):
                        send_heads(qb, g).wait_recv()
            if step < 3:
                compute(N_Z - 1 - step, side)
                compute(1 + step, side)
            elif step < 5:
                compute((4, 0)[step - 3], side)
            for direction in range(2):
                to = lax.rem(z + (N_Z - 1 - step, 1 + step)[direction], N_Z)
                mine = part[side, to, half(direction), :]
                if step:
                    pass_on(direction, step - 1, side).wait_recv()
                    mine = mine + arrived[direction, step - 1, side].astype(f32)
                sent[direction, step, side] = mine.astype(bf16)
                pass_on(direction, step, side).start()

    def total_of(side, direction):
        return part[side, z, half(direction), :] + arrived[direction, N_Z - 2, side].astype(f32)

    is_home = y_lo == y_hi

    def send_last(side, direction):
        slot = jnp.where(is_home, 0, 1) if side else 0
        return pltpu.make_async_remote_copy(
            src_ref=last_sent.at[side, direction],
            dst_ref=last_got.at[slot, direction],
            send_sem=last_send.at[side, direction],
            recv_sem=last_recv.at[slot, direction],
            device_id={"ctx": opposite if side else me, "tp": home},
            device_id_type=MESH,
        )

    def landed(slot, direction):
        return pltpu.make_async_remote_copy(
            src_ref=last_sent.at[slot, direction],
            dst_ref=last_got.at[slot, direction],
            send_sem=last_send.at[slot, direction],
            recv_sem=last_recv.at[slot, direction],
            device_id={"ctx": opposite, "tp": home},
            device_id_type=MESH,
        )

    for direction in range(2):
        pass_on(direction, N_Z - 2, 0).wait_recv()
        last_sent[0, direction] = total_of(0, direction).astype(bf16)

        @pl.when(jnp.logical_not(is_home))
        def _():
            send_last(0, direction).start()

    for direction in range(2):
        pass_on(direction, N_Z - 2, 1).wait_recv()
        last_sent[1, direction] = total_of(1, direction).astype(bf16)
        send_last(1, direction).start()

    @pl.when(jnp.logical_not(is_home))
    def _():
        for direction in range(2):
            landed(0, direction).wait_recv()
            landed(1, direction).wait_recv()
            sum_of_both = last_got[0, direction].astype(f32) + last_got[1, direction].astype(f32)
            out[half(direction), :] = sum_of_both.astype(bf16)
            send_last(0, direction).wait_send()

    @pl.when(is_home)
    def _():
        for direction in range(2):
            landed(0, direction).wait_recv()
            mine = total_of(0, direction) + last_got[0, direction].astype(f32)
            out[half(direction), :] = mine.astype(bf16)

    for rank in range(1, N_CTX):
        ask(rank).wait_send()
        if rank < N_DIRECT + 4:
            send(0, rank).wait_send()
        if rank < N_DIRECT:
            send(1, rank).wait_send()
    send_far_ropes().wait_send()
    swap_far().wait_send()
    for direction in range(2):
        for step in range(4):
            for piece in pieces(direction, step):
                ring(direction, step, piece, seen_from(direction, step)).wait_send()
        for step in range(N_Z - 1):
            for side in range(2):
                pass_on(direction, step, side).wait_send()
    for i in range(8):
        move_w(i).wait_send()
    for qb in range(steps):
        for g in range(heads // group):
            send_heads(qb, g).wait_send()
    for direction in range(2):
        send_last(1, direction).wait_send()


def layer(lists, latent, rope, q_nope, q_rope, w_uk, w_uv, w_out):
    block_groups = latent.shape[1]
    blk = 16 * block_groups
    half, pair = blk // 2, 2 * rope.shape[1] // blk
    queries = q_nope.shape[0]
    heads, dn, dl = w_uk.shape
    dv = w_uv.shape[2]
    steps, blocks = lists.shape
    width, depth = w_out.shape
    asks = (N_CTX, 8, 128)
    vmem = pl.BlockSpec(memory_space=pltpu.VMEM)
    smem = pl.BlockSpec(memory_space=pltpu.SMEM)
    dma = pltpu.SemaphoreType.DMA
    sums = (2, N_Z - 1, 2, width // 2, queries)
    return pl.pallas_call(
        layer_kernel,
        out_shape=jax.ShapeDtypeStruct((width, queries), bf16),
        in_specs=[smem, vmem, vmem] + [pl.BlockSpec(memory_space=pl.ANY)] * 5,
        out_specs=vmem,
        scratch_shapes=[
            pltpu.VMEM(q_nope.shape, bf16),
            pltpu.VMEM(q_rope.shape, bf16),
            pltpu.VMEM(w_uk.shape, bf16),
            pltpu.VMEM(w_uv.shape, bf16),
            dma((5,)),
            pltpu.VMEM((latent.shape[0], half, pair), f32),
            pltpu.VMEM(asks, jnp.int32),
            pltpu.VMEM((steps * blocks, 128), jnp.int32),
            pltpu.SMEM((steps * blocks, 128), jnp.int32),
            pltpu.VMEM(asks, jnp.int32),
            pltpu.SMEM(asks, jnp.int32),
            pltpu.VMEM((N_DIRECT, CAP * block_groups, 16, dl), bf16),
            pltpu.VMEM((4, CAP * block_groups // N_Z, 16, dl), bf16),
            pltpu.VMEM((N_DIRECT, CAP, half, pair), bf16),
            pltpu.VMEM((CAP, half, pair), bf16),
            pltpu.VMEM((N_CTX, CAP * block_groups, 16, dl), bf16),
            pltpu.VMEM((N_CTX, CAP, half, pair), bf16),
            dma((N_CTX,)),
            dma((N_CTX,)),
            dma((N_CTX,)),
            dma((3,)),
            dma((2, N_CTX)),
            dma((2, N_CTX)),
            dma((2, 4, 3)),
            dma((2, 4, 3)),
            pltpu.VMEM((steps, heads, blk, dl + 128), bf16),
            pltpu.VMEM((blocks * blk, dl + 128), bf16),
            pltpu.VMEM((2, queries, heads * dv), bf16),
            dma((steps, 2)),
            dma((steps, 2)),
            pltpu.VMEM((N_Z, width, depth), bf16),
            dma((8,)),
            dma((8,)),
            pltpu.VMEM((2, N_Z, width, queries), f32),
            pltpu.VMEM(sums, bf16),
            pltpu.VMEM(sums, bf16),
            dma(sums[:3]),
            dma(sums[:3]),
            pltpu.VMEM((2, 2, width // 2, queries), bf16),
            pltpu.VMEM((2, 2, width // 2, queries), bf16),
            dma((2, 2)),
            dma((2, 2)),
        ],
        compiler_params=pltpu.CompilerParams(
            collective_id=2, has_side_effects=True, vmem_limit_bytes=VMEM_LIMIT
        ),
    )(lists, latent, rope, q_nope, q_rope, w_uk, w_uv, w_out)


def per_device(q_nope, q_rope, latent, key_rope, w_uk, w_uv, w_out, block_lists):
    per_owner = key_rope.shape[0]
    latent_blocks = latent.reshape(per_owner, -1, 16, latent.shape[1])
    return layer(
        block_lists, latent_blocks, key_rope, q_nope, q_rope, w_uk, w_uv, w_out.T
    ).T


def solution(mesh):
    placed = (
        P("ctx", "tp"),
        P("ctx", "tp"),
        P("ctx", None),
        P("ctx", None),
        P("tp", None, None),
        P("tp", None, None),
        P("tp", "ctx"),
        P("ctx", None),
    )
    return jax.shard_map(
        per_device, mesh=mesh, in_specs=placed, out_specs=P("ctx", "tp"), check_vma=False
    )
```

```python
import functools
import math

import jax
import jax.numpy as jnp
from jax import lax
from jax.experimental import pallas as pl
from jax.experimental.pallas import tpu as pltpu
from jax.sharding import PartitionSpec as P

CAP = 6
N_CTX = 16
N_Z = 8
MESH = pl.DeviceIdType.MESH
bf16 = jnp.bfloat16
f32 = jnp.float32
VMEM_LIMIT = 60 * 1024 * 1024

mscale_sq = (0.1 * math.log(40.0) + 1.0) ** 2


RANKS = [(0, 0), (1, 0), (3, 0), (0, 1), (1, 1), (3, 1), (2, 0), (2, 1)]
N_DIRECT = 8


def shifted(me, dx, dy, dk):
    y, x, core = lax.div(me, 8), lax.rem(lax.div(me, 2), 4), lax.rem(me, 2)
    return lax.rem(y + dy, 2) * 8 + lax.rem(x + dx, 4) * 2 + lax.rem(core + dk, 2)


def owner_of(me, rank):
    dx, dy = RANKS[rank // 2]
    return shifted(me, dx, dy, rank % 2)


def asker_of(me, rank):
    dx, dy = RANKS[rank // 2]
    return shifted(me, (4 - dx) % 4, dy, rank % 2)


def rank_of(owner, me):
    dy = ((owner >> 3) - (me >> 3)) & 1
    dx = ((owner >> 1) - (me >> 1)) & 3
    rank = jnp.zeros_like(owner)
    for i, (x, y) in enumerate(RANKS):
        rank = jnp.where((dx == x) & (dy == y), 2 * i, rank)
    return rank + ((owner - me) & 1)


def sum_lanes(values):
    return jnp.sum(values, axis=1, keepdims=True)


def layer_kernel(
    lists,
    latent_in,
    rope_flat,
    q_nope_in,
    q_rope_in,
    w_uk_in,
    w_uv_in,
    w_out,
    out,
    latent,
    rope_in,
    q_nope,
    q_rope,
    w_uk,
    w_uv,
    load_sems,
    rope,
    offsets,
    table,
    picked,
    got,
    asked,
    direct,
    shared,
    ropes,
    far_ropes,
    kv,
    rp,
    ask_send,
    ask_recv,
    ask_local,
    own_sems,
    ctx_send,
    ctx_recv,
    ring_send,
    ring_recv,
    qbuf,
    kbuf,
    heads_out,
    head_send,
    head_recv,
    w_buf,
    w_send,
    w_recv,
    part,
    sent,
    arrived,
    sum_send,
    sum_recv,
    last_sent,
    last_got,
    last_send,
    last_recv,
):
    me = lax.axis_index("ctx")
    t = lax.axis_index("tp")
    z = lax.rem(t, N_Z)
    y_lo = lax.div(t, N_Z)
    y_hi = lax.div(me, 8)
    x_core = lax.rem(me, 8)
    base = t - z
    right = base + lax.rem(z + 1, N_Z)
    left = base + lax.rem(z + N_Z - 1, N_Z)
    opposite = shifted(me, 0, 1, 0)
    other_core = shifted(me, 0, 0, 1)
    x_next = (shifted(me, 1, 0, 0), shifted(me, 3, 0, 0))
    home = y_hi * N_Z + z
    blk = 16 * latent.shape[1]
    half_blk = blk // 2
    block_groups = blk // 16
    share_groups = CAP * block_groups // N_Z
    heads, dn, dl = w_uk.shape
    dv = w_uv.shape[2]
    dr = q_rope.shape[1] // heads
    steps, blocks = lists.shape
    keys = blocks * blk
    queries = q_nope.shape[0]
    width = w_out.shape[0]
    half_width = width // 2

    barrier = pltpu.get_barrier_semaphore()
    for rank in range(1, N_CTX):
        pl.semaphore_signal(
            barrier, inc=1, device_id={"ctx": owner_of(me, rank)}, device_id_type=MESH
        )
    across = lax.rem(t + N_Z, 2 * N_Z)
    for peer in (left, right, across):
        pl.semaphore_signal(barrier, inc=1, device_id={"tp": peer}, device_id_type=MESH)
    pl.semaphore_signal(
        barrier, inc=1, device_id={"ctx": opposite, "tp": across}, device_id_type=MESH
    )

    own_w = pltpu.make_async_copy(w_out, w_buf.at[x_core], own_sems.at[2])
    own_w.start()
    loads = [
        pltpu.make_async_copy(src, dst, load_sems.at[i])
        for i, (src, dst) in enumerate(
            ((latent_in, latent), (rope_flat, rope_in), (q_nope_in, q_nope), (q_rope_in, q_rope), (w_uk_in, w_uk), (w_uv_in, w_uv))
        )
    ]
    for copy in loads:
        copy.start()


    per_owner = latent.shape[0]
    total_blocks = N_CTX * per_owner
    ids = lax.broadcasted_iota(jnp.int32, (8, total_blocks), 1)
    listed = jnp.zeros((8, total_blocks), jnp.int32)
    for qb in range(steps):
        for j in range(blocks):
            listed = jnp.where(ids == lists[qb, j], 1, listed)
    place_of = listed
    shift = 1
    while shift < per_owner:
        moved = pltpu.roll(place_of, shift, 1)
        place_of = place_of + jnp.where((ids & (per_owner - 1)) >= shift, moved, 0)
        shift *= 2
    place_of = place_of - 1

    owner_row = lax.broadcasted_iota(jnp.int32, (N_CTX, total_blocks), 0)
    lane = lax.broadcasted_iota(jnp.int32, (N_CTX, total_blocks), 1)
    here = (owner_row == (lane >> 5)) & (jnp.broadcast_to(listed[0:1], lane.shape) == 1)
    place_row = jnp.broadcast_to(place_of[0:1], lane.shape)
    small_lane = lax.broadcasted_iota(jnp.int32, (N_CTX, 128), 1)
    wanted = jnp.zeros((N_CTX, 128), jnp.int32)
    for s in range(CAP):
        chosen = sum_lanes(jnp.where(here & (place_row == s), lane & (per_owner - 1), 0))
        wanted = jnp.where(small_lane == s, chosen, wanted)
    offsets[:, 0, :] = wanted

    pl.semaphore_wait(barrier, N_CTX + 3)


    def ask(rank):
        return pltpu.make_async_remote_copy(
            src_ref=offsets.at[owner_of(me, rank)],
            dst_ref=got.at[rank],
            send_sem=ask_send.at[rank],
            recv_sem=ask_recv.at[rank],
            device_id={"ctx": owner_of(me, rank)},
            device_id_type=MESH,
        )

    order = list(range(N_DIRECT, N_CTX)) + list(range(1, N_DIRECT))
    for rank in order:
        ask(rank).start()
    got[0] = offsets[me]


    def to_scalars(rank):
        return pltpu.make_async_copy(got.at[rank], asked.at[rank], ask_local.at[rank])

    far_dy = jnp.where(lax.div(z, 2) == 2, 0, 1)
    far_dx = jnp.where(z < 4, 1 + 2 * lax.div(z, 2), 2)
    far_asker = shifted(me, lax.rem(4 - far_dx, 4), far_dy, lax.rem(z, 2))

    def send(kind, rank):
        if rank >= N_DIRECT:
            src = shared.at[rank - N_DIRECT]
            dst = kv.at[rank, pl.ds(z * share_groups, share_groups)]
        else:
            src, dst = ((direct.at[rank], kv.at[rank]), (ropes.at[rank], rp.at[rank]))[kind]
        return pltpu.make_async_remote_copy(
            src_ref=src,
            dst_ref=dst,
            send_sem=ctx_send.at[kind, rank],
            recv_sem=ctx_recv.at[kind, rank],
            device_id={"ctx": asker_of(me, rank)},
            device_id_type=MESH,
        )

    def send_far_ropes():
        return pltpu.make_async_remote_copy(
            src_ref=far_ropes,
            dst_ref=rp.at[N_DIRECT + z],
            send_sem=ctx_send.at[1, N_DIRECT],
            recv_sem=ctx_recv.at[1, N_DIRECT],
            device_id={"ctx": far_asker},
            device_id_type=MESH,
        )

    for rank in order:
        ask(rank).wait_recv()
        to_scalars(rank).start()
    to_scalars(0).start()
    loads[0].wait()
    for rank in range(N_DIRECT, N_CTX):
        to_scalars(rank).wait()
        for i in range(share_groups):
            group = z * share_groups + i
            block = asked[rank, 0, lax.div(group, block_groups)]
            shared[rank - N_DIRECT, i] = latent[block, lax.rem(group, block_groups)]
        send(0, rank).start()
    loads[1].wait()
    low = lax.broadcasted_iota(jnp.int32, (per_owner, 128), 1) < dr
    for i in range(half_blk):
        at = i // 2 * 128
        first = rope_in[:, at : at + 128].astype(f32)
        second = rope_in[:, half_blk * dr + at : half_blk * dr + at + 128].astype(f32)
        if i % 2:
            first = pltpu.roll(first, dr, 1)
        else:
            second = pltpu.roll(second, dr, 1)
        rope[:, i, :] = jnp.where(low, first, second)

    for s in range(CAP):
        far_ropes[s] = rope[asked[N_DIRECT + z, 0, s]].astype(bf16)
    send_far_ropes().start()
    for rank in list(range(1, N_DIRECT)) + [0]:
        to_scalars(rank).wait()
        for s in range(CAP):
            block = asked[rank, 0, s]
            direct[rank, s * block_groups : (s + 1) * block_groups] = latent[block]
            ropes[rank, s] = rope[block].astype(bf16)
        if rank:
            send(0, rank).start()
            send(1, rank).start()
    own = [
        pltpu.make_async_copy(direct.at[0], kv.at[0], own_sems.at[0]),
        pltpu.make_async_copy(ropes.at[0], rp.at[0], own_sems.at[1]),
    ]
    for copy in own:
        copy.start()


    def ring(direction, step, piece, zz):
        if piece == 2:
            moved = rp.at[N_DIRECT + zz]
        else:
            moved = kv.at[pl.ds(N_DIRECT + 4 * piece, 4), pl.ds(zz * share_groups, share_groups)]
        return pltpu.make_async_remote_copy(
            src_ref=moved,
            dst_ref=moved,
            send_sem=ring_send.at[direction, step, piece],
            recv_sem=ring_recv.at[direction, step, piece],
            device_id={"tp": (right, left)[direction]},
            device_id_type=MESH,
        )

    def pieces(direction, step):
        return (0, 1, 2) if step < 3 else ((0,), (1, 2))[direction]

    def seen_from(direction, step):
        return lax.rem(z + (N_Z - step if direction == 0 else step), N_Z)


    def column(dx):
        return lax.rem(x_core + 2 * dx, 8)

    def move_w(i):
        source = (0, 0, 3, 1, 0, 3, 1, 2)[i]
        rows = pl.ds((i - 2) * half_width, half_width) if i in (2, 3) else pl.ds(0, width)
        peer = other_core if i >= 4 else x_next[i % 2]
        block = w_buf.at[column(source), rows]
        return pltpu.make_async_remote_copy(
            src_ref=block,
            dst_ref=block,
            send_sem=w_send.at[i],
            recv_sem=w_recv.at[i],
            device_id={"ctx": peer},
            device_id_type=MESH,
        )

    for step in range(4):
        for piece in range(3):
            if step == 0:
                if piece == 2:
                    send_far_ropes().wait_recv()
                else:
                    for rank in range(N_DIRECT + 4 * piece, N_DIRECT + 4 * piece + 4):
                        send(0, rank).wait_recv()
            for direction in range(2):
                if step:
                    ring(direction, step - 1, piece, seen_from(direction, step)).wait_recv()
                if piece in pieces(direction, step):
                    ring(direction, step, piece, seen_from(direction, step)).start()
        if step == 0:
            row = lax.broadcasted_iota(jnp.int32, (blocks, total_blocks), 0)
            key_lane = lax.broadcasted_iota(jnp.int32, (blocks, total_blocks), 1)
            places = jnp.broadcast_to(place_of[0:1], key_lane.shape)
            small_row = lax.broadcasted_iota(jnp.int32, (blocks, 128), 0)
            small_lane = lax.broadcasted_iota(jnp.int32, (blocks, 128), 1)
            for qb in range(steps):
                block = jnp.zeros((blocks, 128), jnp.int32)
                for j in range(blocks):
                    block = jnp.where(small_row == j, lists[qb, j], block)
                place = sum_lanes(jnp.where(key_lane == block[:, 0:1], places, 0))
                is_own = block == (total_blocks - N_CTX * steps + me * steps + qb)
                own_at = jnp.max(jnp.where(is_own, small_row * blk, -(1 << 20)), axis=0, keepdims=True)
                rank = rank_of(block >> 5, me)
                entry = jnp.where(small_lane == 0, rank, jnp.where(small_lane == 1, place, own_at))
                table[qb * blocks : (qb + 1) * blocks, :] = entry
            to_picked = pltpu.make_async_copy(table, picked, load_sems.at[6])
            to_picked.start()
            for copy in loads[2:]:
                copy.wait()
            lane = lax.broadcasted_iota(jnp.int32, (queries, 128), 1)
            for h in range(heads):
                up = jnp.dot(q_nope[:, h * dn : (h + 1) * dn], w_uk[h], preferred_element_type=f32)
                qbuf[:, h, :, 0:dl] = up.astype(bf16).reshape(-1, blk, dl)
                pair = q_rope[:, h // 2 * 128 : h // 2 * 128 + 128]
                if h % 2:
                    pair = jnp.concatenate([pair[:, 64:], pair[:, :64]], axis=1)
                pair = jnp.where(lane < dr, pair, jnp.zeros_like(pair))
                qbuf[:, h, :, dl : dl + 128] = pair.reshape(-1, blk, 128)
        if step == 0:
            own_w.wait()
            for i in (0, 1, 4):
                move_w(i).start()
    for direction in range(2):
        for piece in pieces(direction, 3):
            ring(direction, 3, piece, seen_from(direction, 4)).wait_recv()
    for copy in own:
        copy.wait()
    for rank in range(1, N_DIRECT):
        send(0, rank).wait_recv()
        send(1, rank).wait_recv()


    log2_scale = mscale_sq / math.sqrt(dn + dr) * math.log2(math.e)

    group = 4

    def send_heads(qb, g):
        rows = pl.ds(pl.multiple_of(qb * blk, blk), blk)
        columns = pl.ds(g * group * dv, group * dv)
        return pltpu.make_async_remote_copy(
            src_ref=heads_out.at[0, rows, columns],
            dst_ref=heads_out.at[1, rows, columns],
            send_sem=head_send.at[qb, g],
            recv_sem=head_recv.at[qb, g],
            device_id={"ctx": opposite},
            device_id_type=MESH,
        )

    def attend(qb, carry):
        lane = lax.broadcasted_iota(jnp.int32, (half_blk, 128), 1)
        for j in range(blocks):
            rank, place = picked[qb * blocks + j, 0], picked[qb * blocks + j, 1]
            for i in range(block_groups):
                first = j * blk + 16 * i
                kbuf[first : first + 16, 0:dl] = kv[rank, place * block_groups + i]
            pair = rp[rank, place]
            swapped = jnp.concatenate([pair[:, 64:], pair[:, :64]], axis=1)
            zero = jnp.zeros_like(pair)
            kbuf[j * blk : j * blk + half_blk, dl : dl + 128] = jnp.where(lane < dr, pair, zero)
            kbuf[j * blk + half_blk : (j + 1) * blk, dl : dl + 128] = jnp.where(
                lane < dr, swapped, zero
            )
        ahead = lax.broadcasted_iota(jnp.int32, (blk, keys), 1) - picked[qb * blocks, 2]
        row = lax.broadcasted_iota(jnp.int32, (blk, keys), 0)
        bias = jnp.where((ahead > row) & (ahead < blk), f32(-1e30), f32(0.0))

        key = kbuf[...]
        value = key[:, 0:dl]
        rows = pl.ds(pl.multiple_of(qb * blk, blk), blk)
        all_scores = []
        for g in range(heads // group):
            query = qbuf[qb, g * group : (g + 1) * group].reshape(group * blk, dl + 128)
            all_scores.append(
                lax.dot_general(query, key, (((1,), (1,)), ((), ())), preferred_element_type=f32)
            )
        for g in range(heads // group):
            first = g * group
            scores = all_scores[g]
            scores = (scores.reshape(group, blk, keys) + bias[None]).reshape(group * blk, keys)
            top = jnp.max(scores, axis=1, keepdims=True)
            raised = jnp.exp2((scores - top) * log2_scale)
            total = jnp.sum(raised, axis=1, keepdims=True)
            mixed = jnp.dot(raised.astype(bf16), value, preferred_element_type=f32)
            mixed = (mixed / total).astype(bf16).reshape(group, blk, dl)
            for i in range(group):
                h = first + i
                heads_out[0, rows, h * dv : (h + 1) * dv] = jnp.dot(
                    mixed[i], w_uv[h], preferred_element_type=f32
                ).astype(bf16)
            send_heads(qb, g).start()

        @pl.when(qb == 0)
        def _():
            move_w(0).wait_recv()
            move_w(1).wait_recv()
            for i in (2, 3, 5, 6):
                move_w(i).start()

        return carry

    to_picked.wait()
    lax.fori_loop(0, steps, attend, 0)
    move_w(2).wait_recv()
    move_w(3).wait_recv()
    move_w(7).start()
    for i in (4, 5, 6, 7):
        move_w(i).wait_recv()


    def compute(dz, side):
        zz = lax.rem(z + dz, N_Z)
        part[side, zz] = lax.dot_general(
            w_buf[zz], heads_out[side], (((1,), (1,)), ((), ())), preferred_element_type=f32
        )

    def half(direction):
        return slice(direction * half_width, (direction + 1) * half_width)

    def pass_on(direction, step, side):
        return pltpu.make_async_remote_copy(
            src_ref=sent.at[direction, step, side],
            dst_ref=arrived.at[direction, step, side],
            send_sem=sum_send.at[direction, step, side],
            recv_sem=sum_recv.at[direction, step, side],
            device_id={"tp": (right, left)[direction]},
            device_id_type=MESH,
        )

    for step in range(N_Z - 1):
        for side in range(2):
            if step == 0 and side == 1:
                for qb in range(steps):
                    for g in range(heads // group):
                        send_heads(qb, g).wait_recv()
            if step < 3:
                compute(N_Z - 1 - step, side)
                compute(1 + step, side)
            elif step < 5:
                compute((4, 0)[step - 3], side)
            for direction in range(2):
                to = lax.rem(z + (N_Z - 1 - step, 1 + step)[direction], N_Z)
                mine = part[side, to, half(direction), :]
                if step:
                    pass_on(direction, step - 1, side).wait_recv()
                    mine = mine + arrived[direction, step - 1, side].astype(f32)
                sent[direction, step, side] = mine.astype(bf16)
                pass_on(direction, step, side).start()

    def total_of(side, direction):
        return part[side, z, half(direction), :] + arrived[direction, N_Z - 2, side].astype(f32)

    is_home = y_lo == y_hi

    def send_last(side, direction):
        slot = jnp.where(is_home, 0, 1) if side else 0
        return pltpu.make_async_remote_copy(
            src_ref=last_sent.at[side, direction],
            dst_ref=last_got.at[slot, direction],
            send_sem=last_send.at[side, direction],
            recv_sem=last_recv.at[slot, direction],
            device_id={"ctx": opposite if side else me, "tp": home},
            device_id_type=MESH,
        )

    def landed(slot, direction):
        return pltpu.make_async_remote_copy(
            src_ref=last_sent.at[slot, direction],
            dst_ref=last_got.at[slot, direction],
            send_sem=last_send.at[slot, direction],
            recv_sem=last_recv.at[slot, direction],
            device_id={"ctx": opposite, "tp": home},
            device_id_type=MESH,
        )

    for direction in range(2):
        pass_on(direction, N_Z - 2, 0).wait_recv()
        last_sent[0, direction] = total_of(0, direction).astype(bf16)

        @pl.when(jnp.logical_not(is_home))
        def _():
            send_last(0, direction).start()

    for direction in range(2):
        pass_on(direction, N_Z - 2, 1).wait_recv()
        last_sent[1, direction] = total_of(1, direction).astype(bf16)
        send_last(1, direction).start()

    @pl.when(jnp.logical_not(is_home))
    def _():
        for direction in range(2):
            landed(0, direction).wait_recv()
            landed(1, direction).wait_recv()
            sum_of_both = last_got[0, direction].astype(f32) + last_got[1, direction].astype(f32)
            out[half(direction), :] = sum_of_both.astype(bf16)
            send_last(0, direction).wait_send()

    @pl.when(is_home)
    def _():
        for direction in range(2):
            landed(0, direction).wait_recv()
            mine = total_of(0, direction) + last_got[0, direction].astype(f32)
            out[half(direction), :] = mine.astype(bf16)

    for rank in range(1, N_CTX):
        ask(rank).wait_send()
        send(0, rank).wait_send()
        if rank < N_DIRECT:
            send(1, rank).wait_send()
    send_far_ropes().wait_send()
    for direction in range(2):
        for step in range(4):
            for piece in pieces(direction, step):
                ring(direction, step, piece, seen_from(direction, step)).wait_send()
        for step in range(N_Z - 1):
            for side in range(2):
                pass_on(direction, step, side).wait_send()
    for i in range(8):
        move_w(i).wait_send()
    for qb in range(steps):
        for g in range(heads // group):
            send_heads(qb, g).wait_send()
    for direction in range(2):
        send_last(1, direction).wait_send()


def layer(lists, latent, rope, q_nope, q_rope, w_uk, w_uv, w_out):
    block_groups = latent.shape[1]
    blk = 16 * block_groups
    half, pair = blk // 2, 2 * rope.shape[1] // blk
    queries = q_nope.shape[0]
    heads, dn, dl = w_uk.shape
    dv = w_uv.shape[2]
    steps, blocks = lists.shape
    width, depth = w_out.shape
    asks = (N_CTX, 8, 128)
    vmem = pl.BlockSpec(memory_space=pltpu.VMEM)
    smem = pl.BlockSpec(memory_space=pltpu.SMEM)
    dma = pltpu.SemaphoreType.DMA
    sums = (2, N_Z - 1, 2, width // 2, queries)
    return pl.pallas_call(
        layer_kernel,
        out_shape=jax.ShapeDtypeStruct((width, queries), bf16),
        in_specs=[smem] + [pl.BlockSpec(memory_space=pl.ANY)] * 7,
        out_specs=vmem,
        scratch_shapes=[
            pltpu.VMEM(latent.shape, bf16),
            pltpu.VMEM(rope.shape, bf16),
            pltpu.VMEM(q_nope.shape, bf16),
            pltpu.VMEM(q_rope.shape, bf16),
            pltpu.VMEM(w_uk.shape, bf16),
            pltpu.VMEM(w_uv.shape, bf16),
            dma((7,)),
            pltpu.VMEM((latent.shape[0], half, pair), f32),
            pltpu.VMEM(asks, jnp.int32),
            pltpu.VMEM((steps * blocks, 128), jnp.int32),
            pltpu.SMEM((steps * blocks, 128), jnp.int32),
            pltpu.VMEM(asks, jnp.int32),
            pltpu.SMEM(asks, jnp.int32),
            pltpu.VMEM((N_DIRECT, CAP * block_groups, 16, dl), bf16),
            pltpu.VMEM((N_CTX - N_DIRECT, CAP * block_groups // N_Z, 16, dl), bf16),
            pltpu.VMEM((N_DIRECT, CAP, half, pair), bf16),
            pltpu.VMEM((CAP, half, pair), bf16),
            pltpu.VMEM((N_CTX, CAP * block_groups, 16, dl), bf16),
            pltpu.VMEM((N_CTX, CAP, half, pair), bf16),
            dma((N_CTX,)),
            dma((N_CTX,)),
            dma((N_CTX,)),
            dma((3,)),
            dma((2, N_CTX)),
            dma((2, N_CTX)),
            dma((2, 4, 3)),
            dma((2, 4, 3)),
            pltpu.VMEM((steps, heads, blk, dl + 128), bf16),
            pltpu.VMEM((blocks * blk, dl + 128), bf16),
            pltpu.VMEM((2, queries, heads * dv), bf16),
            dma((steps, 2)),
            dma((steps, 2)),
            pltpu.VMEM((N_Z, width, depth), bf16),
            dma((8,)),
            dma((8,)),
            pltpu.VMEM((2, N_Z, width, queries), f32),
            pltpu.VMEM(sums, bf16),
            pltpu.VMEM(sums, bf16),
            dma(sums[:3]),
            dma(sums[:3]),
            pltpu.VMEM((2, 2, width // 2, queries), bf16),
            pltpu.VMEM((2, 2, width // 2, queries), bf16),
            dma((2, 2)),
            dma((2, 2)),
        ],
        compiler_params=pltpu.CompilerParams(
            collective_id=2, has_side_effects=True, vmem_limit_bytes=VMEM_LIMIT
        ),
    )(lists, latent, rope, q_nope, q_rope, w_uk, w_uv, w_out)


def per_device(q_nope, q_rope, latent, key_rope, w_uk, w_uv, w_out, block_lists):
    per_owner = key_rope.shape[0]
    latent_blocks = latent.reshape(per_owner, -1, 16, latent.shape[1])
    return layer(
        block_lists, latent_blocks, key_rope, q_nope, q_rope, w_uk, w_uv, w_out.T
    ).T


def solution(mesh):
    placed = (
        P("ctx", "tp"),
        P("ctx", "tp"),
        P("ctx", None),
        P("ctx", None),
        P("tp", None, None),
        P("tp", None, None),
        P("tp", "ctx"),
        P("ctx", None),
    )
    return jax.shard_map(
        per_device, mesh=mesh, in_specs=placed, out_specs=P("ctx", "tp"), check_vma=False
    )
```

```python
import functools
import math

import jax
import jax.numpy as jnp
from jax import lax
from jax.experimental import pallas as pl
from jax.experimental.pallas import tpu as pltpu
from jax.sharding import PartitionSpec as P

CAP = 6
N_CTX = 16
N_Z = 8
MESH = pl.DeviceIdType.MESH
bf16 = jnp.bfloat16
f32 = jnp.float32
VMEM_LIMIT = 60 * 1024 * 1024

mscale_sq = (0.1 * math.log(40.0) + 1.0) ** 2


RANKS = [(0, 0), (1, 0), (3, 0), (0, 1), (1, 1), (3, 1), (2, 0), (2, 1)]
N_DIRECT = 8


def shifted(me, dx, dy, dk):
    y, x, core = lax.div(me, 8), lax.rem(lax.div(me, 2), 4), lax.rem(me, 2)
    return lax.rem(y + dy, 2) * 8 + lax.rem(x + dx, 4) * 2 + lax.rem(core + dk, 2)


def owner_of(me, rank):
    dx, dy = RANKS[rank // 2]
    return shifted(me, dx, dy, rank % 2)


def asker_of(me, rank):
    dx, dy = RANKS[rank // 2]
    return shifted(me, (4 - dx) % 4, dy, rank % 2)


def rank_of(owner, me):
    dy = ((owner >> 3) - (me >> 3)) & 1
    dx = ((owner >> 1) - (me >> 1)) & 3
    rank = jnp.zeros_like(owner)
    for i, (x, y) in enumerate(RANKS):
        rank = jnp.where((dx == x) & (dy == y), 2 * i, rank)
    return rank + ((owner - me) & 1)


def sum_lanes(values):
    return jnp.sum(values, axis=1, keepdims=True)


def layer_kernel(
    lists,
    latent_in,
    rope_flat,
    q_nope_in,
    q_rope_in,
    w_uk_in,
    w_uv_in,
    w_out,
    out,
    latent,
    rope_in,
    q_nope,
    q_rope,
    w_uk,
    w_uv,
    load_sems,
    rope,
    offsets,
    table,
    picked,
    got,
    asked,
    direct,
    shared,
    ropes,
    far_ropes,
    kv,
    rp,
    ask_send,
    ask_recv,
    ask_local,
    own_sems,
    ctx_send,
    ctx_recv,
    ring_send,
    ring_recv,
    qbuf,
    kbuf,
    heads_out,
    head_send,
    head_recv,
    w_buf,
    w_send,
    w_recv,
    part,
    sent,
    arrived,
    sum_send,
    sum_recv,
    last_sent,
    last_got,
    last_send,
    last_recv,
):
    me = lax.axis_index("ctx")
    t = lax.axis_index("tp")
    z = lax.rem(t, N_Z)
    y_lo = lax.div(t, N_Z)
    y_hi = lax.div(me, 8)
    x_core = lax.rem(me, 8)
    base = t - z
    right = base + lax.rem(z + 1, N_Z)
    left = base + lax.rem(z + N_Z - 1, N_Z)
    opposite = shifted(me, 0, 1, 0)
    other_core = shifted(me, 0, 0, 1)
    x_next = (shifted(me, 1, 0, 0), shifted(me, 3, 0, 0))
    home = y_hi * N_Z + z
    blk = 16 * latent.shape[1]
    half_blk = blk // 2
    block_groups = blk // 16
    share_groups = CAP * block_groups // N_Z
    heads, dn, dl = w_uk.shape
    dv = w_uv.shape[2]
    dr = q_rope.shape[1] // heads
    steps, blocks = lists.shape
    keys = blocks * blk
    queries = q_nope.shape[0]
    width = w_out.shape[0]
    half_width = width // 2

    barrier = pltpu.get_barrier_semaphore()
    for rank in range(1, N_CTX):
        pl.semaphore_signal(
            barrier, inc=1, device_id={"ctx": owner_of(me, rank)}, device_id_type=MESH
        )
    across = lax.rem(t + N_Z, 2 * N_Z)
    for peer in (left, right, across):
        pl.semaphore_signal(barrier, inc=1, device_id={"tp": peer}, device_id_type=MESH)
    pl.semaphore_signal(
        barrier, inc=1, device_id={"ctx": opposite, "tp": across}, device_id_type=MESH
    )

    own_w = pltpu.make_async_copy(w_out, w_buf.at[x_core], own_sems.at[2])
    own_w.start()
    loads = [
        pltpu.make_async_copy(src, dst, load_sems.at[i])
        for i, (src, dst) in enumerate(
            ((latent_in, latent), (rope_flat, rope_in), (q_nope_in, q_nope), (q_rope_in, q_rope), (w_uk_in, w_uk), (w_uv_in, w_uv))
        )
    ]
    for copy in loads:
        copy.start()


    per_owner = latent.shape[0]
    total_blocks = N_CTX * per_owner
    ids = lax.broadcasted_iota(jnp.int32, (8, total_blocks), 1)
    listed = jnp.zeros((8, total_blocks), jnp.int32)
    for qb in range(steps):
        for j in range(blocks):
            listed = jnp.where(ids == lists[qb, j], 1, listed)
    place_of = listed
    shift = 1
    while shift < per_owner:
        moved = pltpu.roll(place_of, shift, 1)
        place_of = place_of + jnp.where((ids & (per_owner - 1)) >= shift, moved, 0)
        shift *= 2
    place_of = place_of - 1

    owner_row = lax.broadcasted_iota(jnp.int32, (N_CTX, total_blocks), 0)
    lane = lax.broadcasted_iota(jnp.int32, (N_CTX, total_blocks), 1)
    here = (owner_row == (lane >> 5)) & (jnp.broadcast_to(listed[0:1], lane.shape) == 1)
    place_row = jnp.broadcast_to(place_of[0:1], lane.shape)
    small_lane = lax.broadcasted_iota(jnp.int32, (N_CTX, 128), 1)
    wanted = jnp.zeros((N_CTX, 128), jnp.int32)
    for s in range(CAP):
        chosen = sum_lanes(jnp.where(here & (place_row == s), lane & (per_owner - 1), 0))
        wanted = jnp.where(small_lane == s, chosen, wanted)
    offsets[:, 0, :] = wanted

    pl.semaphore_wait(barrier, N_CTX + 3)


    def ask(rank):
        return pltpu.make_async_remote_copy(
            src_ref=offsets.at[owner_of(me, rank)],
            dst_ref=got.at[rank],
            send_sem=ask_send.at[rank],
            recv_sem=ask_recv.at[rank],
            device_id={"ctx": owner_of(me, rank)},
            device_id_type=MESH,
        )

    order = list(range(N_DIRECT, N_CTX)) + list(range(1, N_DIRECT))
    for rank in order:
        ask(rank).start()
    got[0] = offsets[me]


    def to_scalars(rank):
        return pltpu.make_async_copy(got.at[rank], asked.at[rank], ask_local.at[rank])

    far_dy = jnp.where(lax.div(z, 2) == 2, 0, 1)
    far_dx = jnp.where(z < 4, 1 + 2 * lax.div(z, 2), 2)
    far_asker = shifted(me, lax.rem(4 - far_dx, 4), far_dy, lax.rem(z, 2))

    def send(kind, rank):
        if rank >= N_DIRECT:
            src = shared.at[rank - N_DIRECT]
            dst = kv.at[rank, pl.ds(z * share_groups, share_groups)]
        else:
            src, dst = ((direct.at[rank], kv.at[rank]), (ropes.at[rank], rp.at[rank]))[kind]
        return pltpu.make_async_remote_copy(
            src_ref=src,
            dst_ref=dst,
            send_sem=ctx_send.at[kind, rank],
            recv_sem=ctx_recv.at[kind, rank],
            device_id={"ctx": asker_of(me, rank)},
            device_id_type=MESH,
        )

    def send_far_ropes():
        return pltpu.make_async_remote_copy(
            src_ref=far_ropes,
            dst_ref=rp.at[N_DIRECT + z],
            send_sem=ctx_send.at[1, N_DIRECT],
            recv_sem=ctx_recv.at[1, N_DIRECT],
            device_id={"ctx": far_asker},
            device_id_type=MESH,
        )

    for rank in order:
        ask(rank).wait_recv()
        to_scalars(rank).start()
    to_scalars(0).start()
    loads[0].wait()
    for rank in range(N_DIRECT, N_CTX):
        to_scalars(rank).wait()
        for i in range(share_groups):
            group = z * share_groups + i
            block = asked[rank, 0, lax.div(group, block_groups)]
            shared[rank - N_DIRECT, i] = latent[block, lax.rem(group, block_groups)]
        send(0, rank).start()
    loads[1].wait()
    low = lax.broadcasted_iota(jnp.int32, (per_owner, 128), 1) < dr
    for i in range(half_blk):
        at = i // 2 * 128
        first = rope_in[:, at : at + 128].astype(f32)
        second = rope_in[:, half_blk * dr + at : half_blk * dr + at + 128].astype(f32)
        if i % 2:
            first = pltpu.roll(first, dr, 1)
        else:
            second = pltpu.roll(second, dr, 1)
        rope[:, i, :] = jnp.where(low, first, second)

    for s in range(CAP):
        far_ropes[s] = rope[asked[N_DIRECT + z, 0, s]].astype(bf16)
    send_far_ropes().start()
    for rank in list(range(1, N_DIRECT)) + [0]:
        to_scalars(rank).wait()
        for s in range(CAP):
            block = asked[rank, 0, s]
            direct[rank, s * block_groups : (s + 1) * block_groups] = latent[block]
            ropes[rank, s] = rope[block].astype(bf16)
        if rank:
            send(0, rank).start()
            send(1, rank).start()
    own = [
        pltpu.make_async_copy(direct.at[0], kv.at[0], own_sems.at[0]),
        pltpu.make_async_copy(ropes.at[0], rp.at[0], own_sems.at[1]),
    ]
    for copy in own:
        copy.start()


    def ring(direction, step, piece, zz):
        if piece == 2:
            moved = rp.at[N_DIRECT + zz]
        else:
            moved = kv.at[pl.ds(N_DIRECT + 4 * piece, 4), pl.ds(zz * share_groups, share_groups)]
        return pltpu.make_async_remote_copy(
            src_ref=moved,
            dst_ref=moved,
            send_sem=ring_send.at[direction, step, piece],
            recv_sem=ring_recv.at[direction, step, piece],
            device_id={"tp": (right, left)[direction]},
            device_id_type=MESH,
        )

    def pieces(direction, step):
        return (0, 1, 2) if step < 3 else ((0,), (1, 2))[direction]

    def seen_from(direction, step):
        return lax.rem(z + (N_Z - step if direction == 0 else step), N_Z)


    def column(dx):
        return lax.rem(x_core + 2 * dx, 8)

    def move_w(i):
        source = (0, 0, 3, 1, 0, 3, 1, 2)[i]
        rows = pl.ds((i - 2) * half_width, half_width) if i in (2, 3) else pl.ds(0, width)
        peer = other_core if i >= 4 else x_next[i % 2]
        block = w_buf.at[column(source), rows]
        return pltpu.make_async_remote_copy(
            src_ref=block,
            dst_ref=block,
            send_sem=w_send.at[i],
            recv_sem=w_recv.at[i],
            device_id={"ctx": peer},
            device_id_type=MESH,
        )

    for step in range(4):
        for piece in range(3):
            if step == 0:
                if piece == 2:
                    send_far_ropes().wait_recv()
                else:
                    for rank in range(N_DIRECT + 4 * piece, N_DIRECT + 4 * piece + 4):
                        send(0, rank).wait_recv()
            for direction in range(2):
                if step:
                    ring(direction, step - 1, piece, seen_from(direction, step)).wait_recv()
                if piece in pieces(direction, step):
                    ring(direction, step, piece, seen_from(direction, step)).start()
        if step == 0:
            own_w.wait()
            for i in (0, 1, 4):
                move_w(i).start()
            row = lax.broadcasted_iota(jnp.int32, (blocks, total_blocks), 0)
            key_lane = lax.broadcasted_iota(jnp.int32, (blocks, total_blocks), 1)
            places = jnp.broadcast_to(place_of[0:1], key_lane.shape)
            small_row = lax.broadcasted_iota(jnp.int32, (blocks, 128), 0)
            small_lane = lax.broadcasted_iota(jnp.int32, (blocks, 128), 1)
            for qb in range(steps):
                block = jnp.zeros((blocks, 128), jnp.int32)
                for j in range(blocks):
                    block = jnp.where(small_row == j, lists[qb, j], block)
                place = sum_lanes(jnp.where(key_lane == block[:, 0:1], places, 0))
                is_own = block == (total_blocks - N_CTX * steps + me * steps + qb)
                own_at = jnp.max(jnp.where(is_own, small_row * blk, -(1 << 20)), axis=0, keepdims=True)
                rank = rank_of(block >> 5, me)
                entry = jnp.where(small_lane == 0, rank, jnp.where(small_lane == 1, place, own_at))
                table[qb * blocks : (qb + 1) * blocks, :] = entry
            to_picked = pltpu.make_async_copy(table, picked, load_sems.at[6])
            to_picked.start()
            for copy in loads[2:]:
                copy.wait()
            lane = lax.broadcasted_iota(jnp.int32, (queries, 128), 1)
            for h in range(heads):
                up = jnp.dot(q_nope[:, h * dn : (h + 1) * dn], w_uk[h], preferred_element_type=f32)
                qbuf[:, h, :, 0:dl] = up.astype(bf16).reshape(-1, blk, dl)
                pair = q_rope[:, h // 2 * 128 : h // 2 * 128 + 128]
                if h % 2:
                    pair = jnp.concatenate([pair[:, 64:], pair[:, :64]], axis=1)
                pair = jnp.where(lane < dr, pair, jnp.zeros_like(pair))
                qbuf[:, h, :, dl : dl + 128] = pair.reshape(-1, blk, 128)
    for direction in range(2):
        for piece in pieces(direction, 3):
            ring(direction, 3, piece, seen_from(direction, 4)).wait_recv()
    for copy in own:
        copy.wait()
    for rank in range(1, N_DIRECT):
        send(0, rank).wait_recv()
        send(1, rank).wait_recv()


    log2_scale = mscale_sq / math.sqrt(dn + dr) * math.log2(math.e)

    group = 4

    def send_heads(qb, g):
        rows = pl.ds(pl.multiple_of(qb * blk, blk), blk)
        columns = pl.ds(g * group * dv, group * dv)
        return pltpu.make_async_remote_copy(
            src_ref=heads_out.at[0, rows, columns],
            dst_ref=heads_out.at[1, rows, columns],
            send_sem=head_send.at[qb, g],
            recv_sem=head_recv.at[qb, g],
            device_id={"ctx": opposite},
            device_id_type=MESH,
        )

    def attend(qb, carry):
        lane = lax.broadcasted_iota(jnp.int32, (half_blk, 128), 1)
        for j in range(blocks):
            rank, place = picked[qb * blocks + j, 0], picked[qb * blocks + j, 1]
            for i in range(block_groups):
                first = j * blk + 16 * i
                kbuf[first : first + 16, 0:dl] = kv[rank, place * block_groups + i]
            pair = rp[rank, place]
            swapped = jnp.concatenate([pair[:, 64:], pair[:, :64]], axis=1)
            zero = jnp.zeros_like(pair)
            kbuf[j * blk : j * blk + half_blk, dl : dl + 128] = jnp.where(lane < dr, pair, zero)
            kbuf[j * blk + half_blk : (j + 1) * blk, dl : dl + 128] = jnp.where(
                lane < dr, swapped, zero
            )
        ahead = lax.broadcasted_iota(jnp.int32, (blk, keys), 1) - picked[qb * blocks, 2]
        row = lax.broadcasted_iota(jnp.int32, (blk, keys), 0)
        bias = jnp.where((ahead > row) & (ahead < blk), f32(-1e30), f32(0.0))

        key = kbuf[...]
        value = key[:, 0:dl]
        rows = pl.ds(pl.multiple_of(qb * blk, blk), blk)
        all_scores = []
        for g in range(heads // group):
            query = qbuf[qb, g * group : (g + 1) * group].reshape(group * blk, dl + 128)
            all_scores.append(
                lax.dot_general(query, key, (((1,), (1,)), ((), ())), preferred_element_type=f32)
            )
        for g in range(heads // group):
            first = g * group
            scores = all_scores[g]
            scores = (scores.reshape(group, blk, keys) + bias[None]).reshape(group * blk, keys)
            top = jnp.max(scores, axis=1, keepdims=True)
            raised = jnp.exp2((scores - top) * log2_scale)
            total = jnp.sum(raised, axis=1, keepdims=True)
            mixed = jnp.dot(raised.astype(bf16), value, preferred_element_type=f32)
            mixed = (mixed / total).astype(bf16).reshape(group, blk, dl)
            for i in range(group):
                h = first + i
                heads_out[0, rows, h * dv : (h + 1) * dv] = jnp.dot(
                    mixed[i], w_uv[h], preferred_element_type=f32
                ).astype(bf16)
            send_heads(qb, g).start()

        @pl.when(qb == 0)
        def _():
            move_w(0).wait_recv()
            move_w(1).wait_recv()
            for i in (2, 3, 5, 6):
                move_w(i).start()

        return carry

    to_picked.wait()
    lax.fori_loop(0, steps, attend, 0)
    move_w(2).wait_recv()
    move_w(3).wait_recv()
    move_w(7).start()
    for i in (4, 5, 6, 7):
        move_w(i).wait_recv()


    def compute(dz, side):
        zz = lax.rem(z + dz, N_Z)
        part[side, zz] = lax.dot_general(
            w_buf[zz], heads_out[side], (((1,), (1,)), ((), ())), preferred_element_type=f32
        )

    def half(direction):
        return slice(direction * half_width, (direction + 1) * half_width)

    def pass_on(direction, step, side):
        return pltpu.make_async_remote_copy(
            src_ref=sent.at[direction, step, side],
            dst_ref=arrived.at[direction, step, side],
            send_sem=sum_send.at[direction, step, side],
            recv_sem=sum_recv.at[direction, step, side],
            device_id={"tp": (right, left)[direction]},
            device_id_type=MESH,
        )

    for step in range(N_Z - 1):
        for side in range(2):
            if step == 0 and side == 1:
                for qb in range(steps):
                    for g in range(heads // group):
                        send_heads(qb, g).wait_recv()
            if step < 3:
                compute(N_Z - 1 - step, side)
                compute(1 + step, side)
            elif step < 5:
                compute((4, 0)[step - 3], side)
            for direction in range(2):
                to = lax.rem(z + (N_Z - 1 - step, 1 + step)[direction], N_Z)
                mine = part[side, to, half(direction), :]
                if step:
                    pass_on(direction, step - 1, side).wait_recv()
                    mine = mine + arrived[direction, step - 1, side].astype(f32)
                sent[direction, step, side] = mine.astype(bf16)
                pass_on(direction, step, side).start()

    def total_of(side, direction):
        return part[side, z, half(direction), :] + arrived[direction, N_Z - 2, side].astype(f32)

    is_home = y_lo == y_hi

    def send_last(side, direction):
        slot = jnp.where(is_home, 0, 1) if side else 0
        return pltpu.make_async_remote_copy(
            src_ref=last_sent.at[side, direction],
            dst_ref=last_got.at[slot, direction],
            send_sem=last_send.at[side, direction],
            recv_sem=last_recv.at[slot, direction],
            device_id={"ctx": opposite if side else me, "tp": home},
            device_id_type=MESH,
        )

    def landed(slot, direction):
        return pltpu.make_async_remote_copy(
            src_ref=last_sent.at[slot, direction],
            dst_ref=last_got.at[slot, direction],
            send_sem=last_send.at[slot, direction],
            recv_sem=last_recv.at[slot, direction],
            device_id={"ctx": opposite, "tp": home},
            device_id_type=MESH,
        )

    for direction in range(2):
        pass_on(direction, N_Z - 2, 0).wait_recv()
        last_sent[0, direction] = total_of(0, direction).astype(bf16)

        @pl.when(jnp.logical_not(is_home))
        def _():
            send_last(0, direction).start()

    for direction in range(2):
        pass_on(direction, N_Z - 2, 1).wait_recv()
        last_sent[1, direction] = total_of(1, direction).astype(bf16)
        send_last(1, direction).start()

    @pl.when(jnp.logical_not(is_home))
    def _():
        for direction in range(2):
            landed(0, direction).wait_recv()
            landed(1, direction).wait_recv()
            sum_of_both = last_got[0, direction].astype(f32) + last_got[1, direction].astype(f32)
            out[half(direction), :] = sum_of_both.astype(bf16)
            send_last(0, direction).wait_send()

    @pl.when(is_home)
    def _():
        for direction in range(2):
            landed(0, direction).wait_recv()
            mine = total_of(0, direction) + last_got[0, direction].astype(f32)
            out[half(direction), :] = mine.astype(bf16)

    for rank in range(1, N_CTX):
        ask(rank).wait_send()
        send(0, rank).wait_send()
        if rank < N_DIRECT:
            send(1, rank).wait_send()
    send_far_ropes().wait_send()
    for direction in range(2):
        for step in range(4):
            for piece in pieces(direction, step):
                ring(direction, step, piece, seen_from(direction, step)).wait_send()
        for step in range(N_Z - 1):
            for side in range(2):
                pass_on(direction, step, side).wait_send()
    for i in range(8):
        move_w(i).wait_send()
    for qb in range(steps):
        for g in range(heads // group):
            send_heads(qb, g).wait_send()
    for direction in range(2):
        send_last(1, direction).wait_send()


def layer(lists, latent, rope, q_nope, q_rope, w_uk, w_uv, w_out):
    block_groups = latent.shape[1]
    blk = 16 * block_groups
    half, pair = blk // 2, 2 * rope.shape[1] // blk
    queries = q_nope.shape[0]
    heads, dn, dl = w_uk.shape
    dv = w_uv.shape[2]
    steps, blocks = lists.shape
    width, depth = w_out.shape
    asks = (N_CTX, 8, 128)
    vmem = pl.BlockSpec(memory_space=pltpu.VMEM)
    smem = pl.BlockSpec(memory_space=pltpu.SMEM)
    dma = pltpu.SemaphoreType.DMA
    sums = (2, N_Z - 1, 2, width // 2, queries)
    return pl.pallas_call(
        layer_kernel,
        out_shape=jax.ShapeDtypeStruct((width, queries), bf16),
        in_specs=[smem] + [pl.BlockSpec(memory_space=pl.ANY)] * 7,
        out_specs=vmem,
        scratch_shapes=[
            pltpu.VMEM(latent.shape, bf16),
            pltpu.VMEM(rope.shape, bf16),
            pltpu.VMEM(q_nope.shape, bf16),
            pltpu.VMEM(q_rope.shape, bf16),
            pltpu.VMEM(w_uk.shape, bf16),
            pltpu.VMEM(w_uv.shape, bf16),
            dma((7,)),
            pltpu.VMEM((latent.shape[0], half, pair), f32),
            pltpu.VMEM(asks, jnp.int32),
            pltpu.VMEM((steps * blocks, 128), jnp.int32),
            pltpu.SMEM((steps * blocks, 128), jnp.int32),
            pltpu.VMEM(asks, jnp.int32),
            pltpu.SMEM(asks, jnp.int32),
            pltpu.VMEM((N_DIRECT, CAP * block_groups, 16, dl), bf16),
            pltpu.VMEM((N_CTX - N_DIRECT, CAP * block_groups // N_Z, 16, dl), bf16),
            pltpu.VMEM((N_DIRECT, CAP, half, pair), bf16),
            pltpu.VMEM((CAP, half, pair), bf16),
            pltpu.VMEM((N_CTX, CAP * block_groups, 16, dl), bf16),
            pltpu.VMEM((N_CTX, CAP, half, pair), bf16),
            dma((N_CTX,)),
            dma((N_CTX,)),
            dma((N_CTX,)),
            dma((3,)),
            dma((2, N_CTX)),
            dma((2, N_CTX)),
            dma((2, 4, 3)),
            dma((2, 4, 3)),
            pltpu.VMEM((steps, heads, blk, dl + 128), bf16),
            pltpu.VMEM((blocks * blk, dl + 128), bf16),
            pltpu.VMEM((2, queries, heads * dv), bf16),
            dma((steps, 2)),
            dma((steps, 2)),
            pltpu.VMEM((N_Z, width, depth), bf16),
            dma((8,)),
            dma((8,)),
            pltpu.VMEM((2, N_Z, width, queries), f32),
            pltpu.VMEM(sums, bf16),
            pltpu.VMEM(sums, bf16),
            dma(sums[:3]),
            dma(sums[:3]),
            pltpu.VMEM((2, 2, width // 2, queries), bf16),
            pltpu.VMEM((2, 2, width // 2, queries), bf16),
            dma((2, 2)),
            dma((2, 2)),
        ],
        compiler_params=pltpu.CompilerParams(
            collective_id=2, has_side_effects=True, vmem_limit_bytes=VMEM_LIMIT
        ),
    )(lists, latent, rope, q_nope, q_rope, w_uk, w_uv, w_out)


def per_device(q_nope, q_rope, latent, key_rope, w_uk, w_uv, w_out, block_lists):
    per_owner = key_rope.shape[0]
    latent_blocks = latent.reshape(per_owner, -1, 16, latent.shape[1])
    return layer(
        block_lists, latent_blocks, key_rope, q_nope, q_rope, w_uk, w_uv, w_out.T
    ).T


def solution(mesh):
    placed = (
        P("ctx", "tp"),
        P("ctx", "tp"),
        P("ctx", None),
        P("ctx", None),
        P("tp", None, None),
        P("tp", None, None),
        P("tp", "ctx"),
        P("ctx", None),
    )
    return jax.shard_map(
        per_device, mesh=mesh, in_specs=placed, out_specs=P("ctx", "tp"), check_vma=False
    )
```
